32 devices in a mesh: gx: 8 (over z, x), gy: 4 (over y, core).
Axes of the slice: x: 2, y: 2, z: 4, core: 2. Of those that a mesh axis runs over, the one named last changes fastest.
Arguments:
- volts_start: float32 [8, 128, 4096], P(None, 'gx', 'gy'), may hold values from 0.55 to 1, as said below
- seg_cond: float32 [8, 128, 4096], P(None, 'gx', 'gy'), may hold values from 0.5 to 2
- via_cond: float32 [7, 128, 4096], P(None, 'gx', 'gy'), may hold values from 1 to 4
- via_mask: int32 [7, 128, 4096], P(None, 'gx', 'gy'), may hold values 0 or 1
- pad_mask: int32 [128, 4096], P('gx', 'gy'), may hold values 0 or 1
- load_current: float32 [128, 4096], P('gx', 'gy'), may hold values from 0 to 2.7, as said below
- stress_start: float32 [8, 128, 4096], P(None, 'gx', 'gy'), may hold values from -6 to 6
- mobility: float32 [8, 128, 4096], P(None, 'gx', 'gy'), may hold values from 0.1 to 0.45
- blocked: int32 [8, 128, 4096], P(None, 'gx', 'gy'), may hold values 0 or 1
- layer_dirs: int32 [8], replicated, may hold values from 0 to 1, as said below
Outputs:
- volts_final: float32 [8, 128, 4096], P(None, 'gx', 'gy')
- stress_final: float32 [8, 128, 4096], P(None, 'gx', 'gy')
- resid_rms: float32 [], replicated
The draws below stay inside these ranges and needn't reach their ends.
Inputs may be any that keep to these rules, and one draw needn't show every extreme that they name: `volts_start`: node voltages near the supply level, one sign. `load_current`: positive load currents. `layer_dirs`: exactly 4 layers run along x and the others along y.
All inputs are finite; a program needn't handle non-finite values. No bound on the sum of `via_mask` or of `pad_mask` or of `blocked` on one device may be relied on, other than what follows from the above.
Results may differ from the reference program's by a relative error of at most 0.00002.
Values sent between devices are 32-bit elements; how exact they have to be, the bound alone decides.
A program may use at most 64 MiB of HBM per device.

```python
import math
import jax
import jax.numpy as jnp

L = 8
SWEEPS = 3
STEPS = 3
NX = 128
NY = 4096


def ramp_pair(strong):
    span_x = jnp.arange(NX, dtype=jnp.float32) / max(NX - 1, 1)
    span_y = jnp.arange(NY, dtype=jnp.float32) / max(NY - 1, 1)
    return (1.0 + strong * span_x)[:, None] * (1.0 + 2.0 * span_y)[None, :]


def draw_volts_start(key, part):
    noise = jax.random.uniform(jax.random.fold_in(key, 11), (L, NX, NY), jnp.float32)
    scale = 0.05 * ramp_pair(2.0)
    return 1.0 - scale[None] * noise


def draw_load_current(key, part):
    noise = jax.random.uniform(jax.random.fold_in(key, 13), (NX, NY), jnp.float32, 0.5, 1.5)
    return 0.1 * ramp_pair(2.0) * noise


def draw_layer_dirs(key, part):
    order = jax.random.permutation(jax.random.fold_in(key, 7), L)
    return (order % 2).astype(jnp.int32)


def with_ends(result, own_key, least, high):
    index_at = [jax.random.randint(jax.random.fold_in(own_key, axis), (), 0, length) for axis, length in enumerate(result.shape)]
    main_axis = result.shape.index(max(result.shape))
    beside = index_at[:main_axis] + [(index_at[main_axis] + 1) % result.shape[main_axis]] + index_at[main_axis + 1:]
    return result.at[tuple(index_at)].set(least).at[tuple(beside)].set(high)


def levels(rng, dims, shards, low, top_value):
    factor_of = 1.0
    for dim, blocks in shards:
        draws = jax.random.uniform(jax.random.fold_in(jax.random.fold_in(rng, 6), dim), (blocks,), jnp.float32, low / len(shards), top_value / len(shards))
        factor_of = factor_of * jnp.repeat(jnp.exp(draws), dims[dim] // blocks).reshape((-1,) + (1,) * (len(dims) - 1 - dim))
    return factor_of


def bell_draw(rng, dims, scale, bound, cuts=(), kind=jnp.bfloat16):
    array = scale * jax.random.normal(rng, dims, jnp.float32)
    if cuts:
        array = array * levels(rng, dims, cuts, -0.22, 0.18)
    return jnp.clip(array, -bound, bound).astype(kind)


def setup_inputs(seed: int = 0) -> dict:
    keys = jax.random.split(jax.random.key(seed), 11)
    return {
        "volts_start": draw_volts_start(jax.random.fold_in(keys[10], 71), 0),
        "seg_cond": jnp.clip(jnp.exp(math.log(2.0) - 1.3862944 * jax.random.uniform(keys[1], (L, NX, NY), jnp.float32) ** levels(keys[1], (L, NX, NY), ((1, 8), (2, 4)), -0.2, 0.2)), 0.5, 2.0),
        "via_cond": jnp.clip(jnp.exp(math.log(4.0) - 1.3862944 * jax.random.uniform(keys[2], (L - 1, NX, NY), jnp.float32) ** levels(keys[2], (L - 1, NX, NY), ((1, 8), (2, 4)), -0.2, 0.2)), 1.0, 4.0),
        "via_mask": with_ends((jax.random.randint(keys[3], (L - 1, NX, NY), 0, 4) < 3).astype(jnp.int32), jax.random.fold_in(keys[3], 1), 0, 1),
        "pad_mask": with_ends((jax.random.randint(keys[4], (NX, NY), 0, 8) < 1).astype(jnp.int32), jax.random.fold_in(keys[4], 1), 0, 1),
        "load_current": draw_load_current(jax.random.fold_in(keys[10], 71), 0),
        "stress_start": bell_draw(keys[6], (L, NX, NY), 1.0, 6.0, ((1, 8), (2, 4)), jnp.float32),
        "mobility": jnp.clip(jnp.exp(math.log(0.45) - 1.50407736 * jax.random.uniform(keys[7], (L, NX, NY), jnp.float32) ** levels(keys[7], (L, NX, NY), ((1, 8), (2, 4)), -0.2, 0.2)), 0.1, 0.45),
        "blocked": with_ends((jax.random.randint(keys[8], (L, NX, NY), 0, 4) < 1).astype(jnp.int32), jax.random.fold_in(keys[8], 1), 0, 1),
        "layer_dirs": draw_layer_dirs(jax.random.fold_in(keys[10], 71), 0),
    }


damping = 0.8
pad_conductance = 4.0
supply_volts = 1.0
wind_factor = 4.0

def prior_x(field):
    return jnp.pad(field, ((0, 0), (1, 0), (0, 0)))[:, :-1, :]

def prior_y(field):
    return jnp.pad(field, ((0, 0), (0, 0), (1, 0)))[:, :, :-1]

def layer_pair(field):
    zero = jnp.zeros_like(field[:1])
    return (jnp.concatenate([zero, field[:-1]], 0), jnp.concatenate([field[1:], zero], 0))

def inflow(volts, cond_xr, cond_yr, via_below, via_above, sources):
    padded = jnp.pad(volts, ((0, 0), (1, 1), (1, 1)))
    below, above = layer_pair(volts)
    total = prior_x(cond_xr) * padded[:, :-2, 1:-1] + cond_xr * padded[:, 2:, 1:-1]
    total = total + prior_y(cond_yr) * padded[:, 1:-1, :-2] + cond_yr * padded[:, 1:-1, 2:]
    return total + via_below * below + via_above * above + sources

def reference(volts_start, seg_cond, via_cond, via_mask, pad_mask, load_current, stress_start, mobility, blocked, layer_dirs):
    layers = seg_cond.shape[0]
    along_y = layer_dirs.astype(jnp.float32)[:, None, None]
    along_x = 1.0 - along_y
    inner_x = (jnp.arange(NX) < NX - 1).astype(jnp.float32)[None, :, None]
    inner_y = (jnp.arange(NY) < NY - 1).astype(jnp.float32)[None, None, :]
    cond_xr = seg_cond * along_x * inner_x
    cond_yr = seg_cond * along_y * inner_y
    via_both = via_cond * via_mask.astype(jnp.float32)
    zero = jnp.zeros((1, NX, NY), jnp.float32)
    via_below = jnp.concatenate([zero, via_both], 0)
    via_above = jnp.concatenate([via_both, zero], 0)
    pads = pad_conductance * pad_mask.astype(jnp.float32)
    level = jnp.arange(layers)[:, None, None]
    top_cond = jnp.where(level == layers - 1, pads[None], jnp.float32(0.0))
    sources = top_cond * supply_volts - jnp.where(level == 0, load_current[None], jnp.float32(0.0))
    diagonal = prior_x(cond_xr) + cond_xr + prior_y(cond_yr) + cond_yr + via_below + via_above + top_cond
    volts = volts_start
    for sweep in range(SWEEPS):
        volts = (1.0 - damping) * volts + damping * inflow(volts, cond_xr, cond_yr, via_below, via_above, sources) / diagonal
    resid = inflow(volts, cond_xr, cond_yr, via_below, via_above, sources) - diagonal * volts
    resid_rms = jnp.sqrt(jnp.sum(resid * resid) / (layers * NX * NY))
    padded = jnp.pad(volts, ((0, 0), (1, 1), (1, 1)))
    current_x = cond_xr * (volts - padded[:, 2:, 1:-1])
    current_y = cond_yr * (volts - padded[:, 1:-1, 2:])
    open_seg = 1.0 - blocked.astype(jnp.float32)
    mobile_x = mobility * open_seg * along_x * inner_x
    mobile_y = mobility * open_seg * along_y * inner_y
    wind_x = mobile_x * wind_factor * current_x
    wind_y = mobile_y * wind_factor * current_y
    drift = wind_x - prior_x(wind_x) + wind_y - prior_y(wind_y)
    mobile_xl = prior_x(mobile_x)
    mobile_yl = prior_y(mobile_y)
    stress = stress_start
    for step in range(STEPS):
        padded = jnp.pad(stress, ((0, 0), (1, 1), (1, 1)))
        stress = stress + mobile_x * (padded[:, 2:, 1:-1] - stress) - mobile_xl * (stress - padded[:, :-2, 1:-1]) + mobile_y * (padded[:, 1:-1, 2:] - stress) - mobile_yl * (stress - padded[:, 1:-1, :-2]) + drift
    return (volts, stress, resid_rms)
```

```python
import functools
import jax
import jax.numpy as jnp
from jax import lax
from jax.experimental import pallas as pl
from jax.experimental.pallas import tpu as pltpu
from jax.sharding import PartitionSpec as P

damping = 0.8
pad_conductance = 4.0
supply_volts = 1.0
wind_factor = 4.0

MESH = pl.DeviceIdType.MESH
VOLTS, STRESS, PARTIAL, VOLTS2, STRESS1 = range(5)
ROUNDS = 5


def kernel(
    n_x, n_y, layers, rows_x, rows_y,
    dirs, volts_hbm, seg_hbm, via_hbm, vmask_hbm, pad_hbm, load_hbm, stress_hbm, mob_hbm, blk_hbm,
    volts_out, stress_out, rms_out,
    volts_in, seg_in, via_in, vmask_in, pad_in, load_in, stress_in, mob_in, blk_in,
    cond_r, cond_l, via_b, via_a, source, diag, weight, partial,
    mob_r, mob_l, wind_r, wind_l, volts_a, volts_b, stress_a, volts_fin, stress_fin,
    send_x, recv_x, send_y, recv_y, sum_x, sum_y,
    in_sem, out_sem, send_sem, recv_sem, sx_send, sx_recv, sy_send, sy_recv,
):
    half = layers // 2
    gx = lax.axis_index("gx")
    gy = lax.axis_index("gy")

    moves = [
        pltpu.make_async_copy(src, dst, in_sem.at[i])
        for i, (src, dst) in enumerate(
            [
                (volts_hbm, volts_in), (seg_hbm, seg_in), (via_hbm, via_in), (vmask_hbm, vmask_in), (pad_hbm, pad_in),
                (load_hbm, load_in), (stress_hbm, stress_in), (mob_hbm, mob_in), (blk_hbm, blk_in),
            ]
        )
    ]
    for move in moves:
        move.start()

    barrier = pltpu.get_barrier_semaphore()
    for o in range(1, n_x):
        pl.semaphore_signal(barrier, inc=1, device_id=(lax.rem(gx + o, n_x), gy), device_id_type=MESH)
    for o in range(1, n_y):
        pl.semaphore_signal(barrier, inc=1, device_id=(gx, lax.rem(gy + o, n_y)), device_id_type=MESH)

    to_has = [gx < n_x - 1, gx > 0, gy < n_y - 1, gy > 0]
    from_has = [gx > 0, gx < n_x - 1, gy > 0, gy < n_y - 1]
    target = [
        (jnp.minimum(gx + 1, n_x - 1), gy), (jnp.maximum(gx - 1, 0), gy),
        (gx, jnp.minimum(gy + 1, n_y - 1)), (gx, jnp.maximum(gy - 1, 0)),
    ]

    def edge_copy(r, d):
        if d < 2:
            count = 1 if (d == 1 and r in (VOLTS, STRESS)) else 2
            src, dst = send_x.at[r, d, 0:count], recv_x.at[r, d, 0:count]
        else:
            src, dst = send_y.at[r, d - 2], recv_y.at[r, d - 2]
        return pltpu.make_async_remote_copy(
            src_ref=src, dst_ref=dst, send_sem=send_sem.at[r, d], recv_sem=recv_sem.at[r, d],
            device_id=target[d], device_id_type=MESH,
        )

    def start(r):
        for d in range(4):
            @pl.when(to_has[d])
            def _():
                edge_copy(r, d).start()

    def arrive(r):
        for d in range(4):
            @pl.when(from_has[d])
            def _():
                edge_copy(r, d).wait_recv()

    for d in range(2):
        @pl.when(jnp.logical_not(from_has[d]))
        def _():
            for r in range(ROUNDS):
                recv_x[r, d] = jnp.full(recv_x.shape[2:], 1.0 if r == PARTIAL else 0.0, jnp.float32)

        @pl.when(jnp.logical_not(from_has[d + 2]))
        def _():
            for r in range(ROUNDS):
                recv_y[r, d] = jnp.full(recv_y.shape[2:], 1.0 if r == PARTIAL else 0.0, jnp.float32)

    is_y = [dirs[l] for l in range(layers)]
    pos = []
    seen_x, seen_y = jnp.int32(0), jnp.int32(half)
    for l in range(layers):
        pos.append(jnp.where(is_y[l] == 1, seen_y, seen_x))
        seen_y = seen_y + is_y[l]
        seen_x = seen_x + 1 - is_y[l]
    layer = []
    for k in range(layers):
        at = jnp.int32(0)
        for l in range(1, layers):
            at = at + jnp.where(pos[l] == k, l, 0)
        layer.append(at)

    def slot_of(want):
        at = jnp.int32(0)
        for k in range(1, layers):
            at = at + jnp.where(layer[k] == want, k, 0)
        return at

    below = [jnp.maximum(layer[k] - 1, 0) for k in range(layers)]
    above = [jnp.minimum(layer[k] + 1, layers - 1) for k in range(layers)]
    slot_below = [slot_of(below[k]) for k in range(layers)]
    slot_above = [slot_of(above[k]) for k in range(layers)]

    shape = (rows_x, rows_y)
    index = [lax.broadcasted_iota(jnp.int32, shape, 0), lax.broadcasted_iota(jnp.int32, shape, 1)]
    length = [rows_x, rows_y]
    is_first = [index[0] == 0, index[1] == 0]
    is_last = [index[0] == rows_x - 1, index[1] == rows_y - 1]
    outer = [
        jnp.logical_and(is_last[0], gx == n_x - 1),
        jnp.logical_and(is_last[1], gy == n_y - 1),
    ]
    lane = lax.broadcasted_iota(jnp.int32, (rows_x, 128), 1)

    def axis_of(k):
        return 0 if k < half else 1

    def before(a, h, axis):
        return jnp.where(is_first[axis], h, pltpu.roll(a, 1, axis))

    def after(a, h, axis):
        return jnp.where(is_last[axis], h, pltpu.roll(a, length[axis] - 1, axis))

    def first(a, axis):
        return a[0:1, :] if axis == 0 else a[:, 0:1]

    def last(a, axis):
        return a[rows_x - 1:rows_x, :] if axis == 0 else a[:, rows_y - 1:rows_y]

    def put(r, k, to_next, to_prev):
        for d, values in ((0, to_next), (1, to_prev)):
            if k < half:
                for i, value in enumerate(values):
                    send_x[r, d, i, k:k + 1, :] = value
            else:
                packed = jnp.broadcast_to(values[0], (rows_x, 128))
                if len(values) > 1:
                    packed = jnp.where(lane == 0, packed, values[1])
                send_y[r, d, k - half] = packed

    def halo(r, k, d, i):
        if k < half:
            return recv_x[r, d, i, k:k + 1, :]
        return recv_y[r, d, k - half, :, i:i + 1]

    moves[0].wait()
    moves[1].wait()
    for k in range(layers):
        axis = axis_of(k)
        cr = jnp.where(outer[axis], 0.0, seg_in[layer[k]])
        cond_r[k] = cr
        cond_l[k] = before(cr, 0.0, axis)
        v = volts_in[layer[k]]
        put(VOLTS, k, [last(v, axis), last(cr, axis)], [first(v, axis)])
    pl.semaphore_wait(barrier, n_x + n_y - 2)
    start(VOLTS)

    for move in moves[2:6]:
        move.wait()
    pads = pad_conductance * pad_in[...].astype(jnp.float32)
    load = load_in[...]
    for k in range(layers):
        axis = axis_of(k)
        l = layer[k]
        up = jnp.minimum(l, layers - 2)
        va = via_in[up] * vmask_in[up].astype(jnp.float32) * jnp.where(l < layers - 1, 1.0, 0.0)
        vb = via_in[below[k]] * vmask_in[below[k]].astype(jnp.float32) * jnp.where(l > 0, 1.0, 0.0)
        top = pads * jnp.where(l == layers - 1, 1.0, 0.0)
        src = top * supply_volts - load * jnp.where(l == 0, 1.0, 0.0)
        via_a[k] = va
        via_b[k] = vb
        source[k] = src
        v = volts_in[l]
        cl, cr = cond_l[k], cond_r[k]
        dg = cl + cr + va + vb + top
        num = cl * before(v, 0.0, axis) + cr * after(v, 0.0, axis) + vb * volts_in[below[k]] + va * volts_in[above[k]] + src
        diag[k] = dg
        partial[k] = num
        put(PARTIAL, k, [last(num, axis), last(dg, axis)], [first(num, axis), first(dg, axis)])
    start(PARTIAL)

    for move in moves[6:]:
        move.wait()
    for k in range(layers):
        axis = axis_of(k)
        l = layer[k]
        mr = jnp.where(outer[axis], 0.0, mob_in[l] * (1.0 - blk_in[l].astype(jnp.float32)))
        mob_r[k] = mr
        s = stress_in[l]
        put(STRESS, k, [last(s, axis), last(mr, axis)], [first(s, axis)])
    start(STRESS)

    def edge_next(k, v_prev, n_prev, v_next, n_next, v):
        axis = axis_of(k)
        c_in, c_out = halo(VOLTS, k, 0, 1), last(cond_r[k], axis)
        h_prev = (1.0 - damping) * v_prev + damping * (n_prev + c_in * first(v, axis)) / halo(PARTIAL, k, 0, 1)
        h_next = (1.0 - damping) * v_next + damping * (n_next + c_out * last(v, axis)) / (halo(PARTIAL, k, 1, 1) + c_out)
        return h_prev, h_next

    arrive(VOLTS)
    for k in range(layers):
        axis = axis_of(k)
        c_in = halo(VOLTS, k, 0, 1)
        cl = jnp.where(is_first[axis], c_in, cond_l[k])
        cond_l[k] = cl
        dg = diag[k] + jnp.where(is_first[axis], c_in, 0.0)
        diag[k] = dg
        w = damping / dg
        weight[k] = w
        num = partial[k] + jnp.where(is_first[axis], c_in * halo(VOLTS, k, 0, 0), 0.0)
        num = num + jnp.where(is_last[axis], cond_r[k] * halo(VOLTS, k, 1, 0), 0.0)
        volts_a[k] = (1.0 - damping) * volts_in[layer[k]] + w * num

    def inflow(v_ref, k, v, h_prev, h_next):
        axis = axis_of(k)
        lateral = cond_l[k] * before(v, h_prev, axis) + cond_r[k] * after(v, h_next, axis)
        return lateral + via_b[k] * v_ref[slot_below[k]] + via_a[k] * v_ref[slot_above[k]] + source[k]

    arrive(PARTIAL)
    for k in range(layers):
        v = volts_a[k]
        h_prev, h_next = edge_next(
            k, halo(VOLTS, k, 0, 0), halo(PARTIAL, k, 0, 0), halo(VOLTS, k, 1, 0), halo(PARTIAL, k, 1, 0),
            volts_in[layer[k]],
        )
        volts_b[k] = (1.0 - damping) * v + weight[k] * inflow(volts_a, k, v, h_prev, h_next)
    for k in range(layers):
        axis = axis_of(k)
        v = volts_b[k]
        num = inflow(volts_b, k, v, 0.0, 0.0)
        partial[k] = num
        put(VOLTS2, k, [last(v, axis), last(num, axis)], [first(v, axis), first(num, axis)])
    start(VOLTS2)

    arrive(STRESS)
    for k in range(layers):
        axis = axis_of(k)
        mr = mob_r[k]
        ml = before(mr, halo(STRESS, k, 0, 1), axis)
        mob_l[k] = ml
        wind_r[k] = wind_factor * mr * cond_r[k]
        wind_l[k] = wind_factor * ml * cond_l[k]

    arrive(VOLTS2)
    for k in range(layers):
        axis = axis_of(k)
        num = partial[k] + jnp.where(is_first[axis], cond_l[k] * halo(VOLTS2, k, 0, 0), 0.0)
        num = num + jnp.where(is_last[axis], cond_r[k] * halo(VOLTS2, k, 1, 0), 0.0)
        volts_a[k] = (1.0 - damping) * volts_b[k] + weight[k] * num

    total = jnp.zeros(shape, jnp.float32)
    for k in range(layers):
        axis = axis_of(k)
        v = volts_a[k]
        h_prev, h_next = edge_next(
            k, halo(VOLTS2, k, 0, 0), halo(VOLTS2, k, 0, 1), halo(VOLTS2, k, 1, 0), halo(VOLTS2, k, 1, 1), volts_b[k]
        )
        v_prev, v_next = before(v, h_prev, axis), after(v, h_next, axis)
        resid = cond_l[k] * v_prev + cond_r[k] * v_next + via_b[k] * volts_a[slot_below[k]]
        resid = resid + via_a[k] * volts_a[slot_above[k]] + source[k] - diag[k] * v
        total = total + resid * resid
        drift = wind_r[k] * (v - v_next) - wind_l[k] * (v_prev - v)
        mr, ml = mob_r[k], mob_l[k]
        s = stress_in[layer[k]]
        s_prev, s_next = before(s, halo(STRESS, k, 0, 0), axis), after(s, halo(STRESS, k, 1, 0), axis)
        s = s + mr * (s_next - s) - ml * (s - s_prev) + drift
        stress_a[k] = s
        part = s + mr * (after(s, 0.0, axis) - s) - ml * (s - before(s, 0.0, axis)) + drift
        partial[k] = part
        weight[k] = drift
        put(STRESS1, k, [last(s, axis), last(part, axis)], [first(s, axis), first(part, axis)])
    start(STRESS1)

    def sum_copy(group, sem_s, sem_r, o, axis, sender):
        me, n = (gx, n_x) if axis == 0 else (gy, n_y)
        other = lax.rem(me + o, n)
        slot = me if sender else other
        return pltpu.make_async_remote_copy(
            src_ref=group.at[me], dst_ref=group.at[slot], send_sem=sem_s.at[o - 1], recv_sem=sem_r.at[slot],
            device_id=(other, gy) if axis == 0 else (gx, other), device_id_type=MESH,
        )

    def fold(a):
        r = a[0:8]
        for i in range(8, a.shape[0], 8):
            r = r + a[i:i + 8]
        out = r[:, 0:128]
        for j in range(128, a.shape[1], 128):
            out = out + r[:, j:j + 128]
        return out

    sum_x[gx] = fold(total)
    for o in range(1, n_x):
        sum_copy(sum_x, sx_send, sx_recv, o, 0, True).start()

    for l in range(layers):
        volts_fin[l] = volts_a[pos[l]]
    out_v = pltpu.make_async_copy(volts_fin, volts_out, out_sem.at[0])
    out_v.start()

    for o in range(1, n_x):
        sum_copy(sum_x, sx_send, sx_recv, o, 0, False).wait_recv()
    along = sum_x[0]
    for i in range(1, n_x):
        along = along + sum_x[i]
    sum_y[gy] = along
    for o in range(1, n_y):
        sum_copy(sum_y, sy_send, sy_recv, o, 1, True).start()

    arrive(STRESS1)
    for k in range(layers):
        axis = axis_of(k)
        mr, ml, s1 = mob_r[k], mob_l[k], stress_a[k]
        m_in, m_out = first(ml, axis), last(mr, axis)
        s_prev, s_next = halo(STRESS1, k, 0, 0), halo(STRESS1, k, 1, 0)
        s = partial[k] + jnp.where(is_first[axis], ml * s_prev, 0.0) + jnp.where(is_last[axis], mr * s_next, 0.0)
        h_prev = halo(STRESS1, k, 0, 1) + m_in * first(s1, axis)
        h_next = halo(STRESS1, k, 1, 1) + m_out * last(s1, axis)
        s = s + mr * (after(s, h_next, axis) - s) - ml * (s - before(s, h_prev, axis)) + weight[k]
        stress_a[k] = s
    for l in range(layers):
        stress_fin[l] = stress_a[pos[l]]
    out_s = pltpu.make_async_copy(stress_fin, stress_out, out_sem.at[1])
    out_s.start()

    for o in range(1, n_y):
        sum_copy(sum_y, sy_send, sy_recv, o, 1, False).wait_recv()
    whole = sum_y[0]
    for i in range(1, n_y):
        whole = whole + sum_y[i]
    nodes = layers * n_x * rows_x * n_y * rows_y
    mean = jnp.sum(whole, keepdims=True) * (1.0 / nodes)
    rms_out[0, 0] = jnp.sqrt(mean)[0, 0]

    for r in range(ROUNDS):
        for d in range(4):
            @pl.when(to_has[d])
            def _():
                edge_copy(r, d).wait_send()
    for o in range(1, n_x):
        sum_copy(sum_x, sx_send, sx_recv, o, 0, True).wait_send()
    for o in range(1, n_y):
        sum_copy(sum_y, sy_send, sy_recv, o, 1, True).wait_send()
    out_v.wait()
    out_s.wait()


def body(n_x, n_y, volts_start, seg_cond, via_cond, via_mask, pad_mask, load_current, stress_start, mobility, blocked, layer_dirs):
    layers, rows_x, rows_y = seg_cond.shape
    half = layers // 2
    f32, i32 = jnp.float32, jnp.int32
    full = (layers, rows_x, rows_y)
    vias = via_cond.shape
    flat = (rows_x, rows_y)
    dma = pltpu.SemaphoreType.DMA
    hbm = pl.BlockSpec(memory_space=pl.ANY)
    volts, stress, rms = pl.pallas_call(
        functools.partial(kernel, n_x, n_y, layers, rows_x, rows_y),
        out_shape=(
            jax.ShapeDtypeStruct(full, f32),
            jax.ShapeDtypeStruct(full, f32),
            jax.ShapeDtypeStruct((1, 1), f32),
        ),
        in_specs=[pl.BlockSpec(memory_space=pltpu.SMEM)] + [hbm] * 9,
        out_specs=(hbm, hbm, pl.BlockSpec(memory_space=pltpu.SMEM)),
        scratch_shapes=[
            pltpu.VMEM(full, f32), pltpu.VMEM(full, f32), pltpu.VMEM(vias, f32), pltpu.VMEM(vias, i32),
            pltpu.VMEM(flat, i32), pltpu.VMEM(flat, f32), pltpu.VMEM(full, f32), pltpu.VMEM(full, f32), pltpu.VMEM(full, i32),
        ]
        + [pltpu.VMEM(full, f32)] * 17
        + [
            pltpu.VMEM((ROUNDS, 2, 2, half, rows_y), f32), pltpu.VMEM((ROUNDS, 2, 2, half, rows_y), f32),
            pltpu.VMEM((ROUNDS, 2, half, rows_x, 128), f32), pltpu.VMEM((ROUNDS, 2, half, rows_x, 128), f32),
            pltpu.VMEM((n_x, 8, 128), f32), pltpu.VMEM((n_y, 8, 128), f32),
            dma((9,)), dma((2,)), dma((ROUNDS, 4)), dma((ROUNDS, 4)),
            dma((n_x,)), dma((n_x,)), dma((n_y,)), dma((n_y,)),
        ],
        compiler_params=pltpu.CompilerParams(
            collective_id=0, has_side_effects=True, vmem_limit_bytes=40 * 1024 * 1024
        ),
        cost_estimate=pl.CostEstimate(flops=20_000_000, bytes_accessed=5_000_000, transcendentals=0),
    )(layer_dirs, volts_start, seg_cond, via_cond, via_mask, pad_mask, load_current, stress_start, mobility, blocked)
    return volts, stress, rms.reshape(())


def solution(mesh):
    tile = P(None, "gx", "gy")
    flat = P("gx", "gy")
    in_specs = (tile, tile, tile, tile, flat, flat, tile, tile, tile, P())
    return jax.shard_map(
        functools.partial(body, mesh.shape["gx"], mesh.shape["gy"]),
        mesh=mesh, in_specs=in_specs, out_specs=(tile, tile, P()), check_vma=False,
    )
```

```python
import functools
import jax
import jax.numpy as jnp
from jax import lax
from jax.experimental import pallas as pl
from jax.experimental.pallas import tpu as pltpu
from jax.sharding import PartitionSpec as P

damping = 0.8
pad_conductance = 4.0
supply_volts = 1.0
wind_factor = 4.0

MESH = pl.DeviceIdType.MESH
VOLTS, STRESS, PARTIAL, VOLTS2, STRESS1 = range(5)
ROUNDS = 5


def kernel(
    n_x, n_y, layers, rows_x, rows_y,
    dirs_hbm, volts_hbm, seg_hbm, via_hbm, vmask_hbm, pad_hbm, load_hbm, stress_hbm, mob_hbm, blk_hbm,
    volts_out, stress_out, rms_out,
    dirs, volts_in, seg_in, via_in, vmask_in, pad_in, load_in, stress_in, mob_in, blk_in,
    cond_r, cond_l, via_b, via_a, source, diag, weight, partial,
    mob_r, mob_l, wind_r, wind_l, volts_a, volts_b, stress_a, volts_fin, stress_fin,
    send_x, recv_x, send_y, recv_y, sum_x, sum_y,
    in_sem, out_sem, send_sem, recv_sem, sx_send, sx_recv, sy_send, sy_recv,
):
    half = layers // 2
    gx = lax.axis_index("gx")
    gy = lax.axis_index("gy")

    moves = [
        pltpu.make_async_copy(src, dst, in_sem.at[i])
        for i, (src, dst) in enumerate(
            [
                (volts_hbm, volts_in), (seg_hbm, seg_in), (via_hbm, via_in), (vmask_hbm, vmask_in), (pad_hbm, pad_in),
                (load_hbm, load_in), (stress_hbm, stress_in), (mob_hbm, mob_in), (blk_hbm, blk_in), (dirs_hbm, dirs),
            ]
        )
    ]
    moves[9].start()
    for move in moves[:9]:
        move.start()

    barrier = pltpu.get_barrier_semaphore()
    for o in range(1, n_x):
        pl.semaphore_signal(barrier, inc=1, device_id=(lax.rem(gx + o, n_x), gy), device_id_type=MESH)
    for o in range(1, n_y):
        pl.semaphore_signal(barrier, inc=1, device_id=(gx, lax.rem(gy + o, n_y)), device_id_type=MESH)

    to_has = [gx < n_x - 1, gx > 0, gy < n_y - 1, gy > 0]
    from_has = [gx > 0, gx < n_x - 1, gy > 0, gy < n_y - 1]
    target = [
        (jnp.minimum(gx + 1, n_x - 1), gy), (jnp.maximum(gx - 1, 0), gy),
        (gx, jnp.minimum(gy + 1, n_y - 1)), (gx, jnp.maximum(gy - 1, 0)),
    ]

    def edge_copy(r, d):
        if d < 2:
            count = 1 if (d == 1 and r in (VOLTS, STRESS)) else 2
            src, dst = send_x.at[r, d, 0:count], recv_x.at[r, d, 0:count]
        else:
            src, dst = send_y.at[r, d - 2], recv_y.at[r, d - 2]
        return pltpu.make_async_remote_copy(
            src_ref=src, dst_ref=dst, send_sem=send_sem.at[r, d], recv_sem=recv_sem.at[r, d],
            device_id=target[d], device_id_type=MESH,
        )

    def start(r, axis):
        for d in (2 * axis, 2 * axis + 1):
            @pl.when(to_has[d])
            def _():
                edge_copy(r, d).start()

    def arrive(r):
        for d in range(4):
            @pl.when(from_has[d])
            def _():
                edge_copy(r, d).wait_recv()

    for d in range(2):
        @pl.when(jnp.logical_not(from_has[d]))
        def _():
            for r in range(ROUNDS):
                recv_x[r, d] = jnp.full(recv_x.shape[2:], 1.0 if r == PARTIAL else 0.0, jnp.float32)

        @pl.when(jnp.logical_not(from_has[d + 2]))
        def _():
            for r in range(ROUNDS):
                recv_y[r, d] = jnp.full(recv_y.shape[2:], 1.0 if r == PARTIAL else 0.0, jnp.float32)

    moves[9].wait()
    is_y = [dirs[l] for l in range(layers)]
    pos = []
    seen_x, seen_y = jnp.int32(0), jnp.int32(half)
    for l in range(layers):
        pos.append(jnp.where(is_y[l] == 1, seen_y, seen_x))
        seen_y = seen_y + is_y[l]
        seen_x = seen_x + 1 - is_y[l]
    layer = []
    for k in range(layers):
        at = jnp.int32(0)
        for l in range(1, layers):
            at = at + jnp.where(pos[l] == k, l, 0)
        layer.append(at)

    def slot_of(want):
        at = jnp.int32(0)
        for k in range(1, layers):
            at = at + jnp.where(layer[k] == want, k, 0)
        return at

    below = [jnp.maximum(layer[k] - 1, 0) for k in range(layers)]
    above = [jnp.minimum(layer[k] + 1, layers - 1) for k in range(layers)]
    slot_below = [slot_of(below[k]) for k in range(layers)]
    slot_above = [slot_of(above[k]) for k in range(layers)]

    shape = (rows_x, rows_y)
    index = [lax.broadcasted_iota(jnp.int32, shape, 0), lax.broadcasted_iota(jnp.int32, shape, 1)]
    length = [rows_x, rows_y]
    is_first = [index[0] == 0, index[1] == 0]
    is_last = [index[0] == rows_x - 1, index[1] == rows_y - 1]
    outer = [
        jnp.logical_and(is_last[0], gx == n_x - 1),
        jnp.logical_and(is_last[1], gy == n_y - 1),
    ]
    lane = lax.broadcasted_iota(jnp.int32, (rows_x, 128), 1)

    def axis_of(k):
        return 0 if k < half else 1

    def before(a, h, axis):
        return jnp.where(is_first[axis], h, pltpu.roll(a, 1, axis))

    def after(a, h, axis):
        return jnp.where(is_last[axis], h, pltpu.roll(a, length[axis] - 1, axis))

    def first(a, axis):
        return a[0:1, :] if axis == 0 else a[:, 0:1]

    def last(a, axis):
        return a[rows_x - 1:rows_x, :] if axis == 0 else a[:, rows_y - 1:rows_y]

    def put(r, k, to_next, to_prev):
        for d, values in ((0, to_next), (1, to_prev)):
            if k < half:
                for i, value in enumerate(values):
                    send_x[r, d, i, k:k + 1, :] = value
            else:
                packed = jnp.broadcast_to(values[0], (rows_x, 128))
                if len(values) > 1:
                    packed = jnp.where(lane == 0, packed, values[1])
                send_y[r, d, k - half] = packed

    def halo(r, k, d, i):
        if k < half:
            return recv_x[r, d, i, k:k + 1, :]
        return recv_y[r, d, k - half, :, i:i + 1]

    moves[0].wait()
    moves[1].wait()
    for k in range(layers):
        axis = axis_of(k)
        cr = jnp.where(outer[axis], 0.0, seg_in[layer[k]])
        cond_r[k] = cr
        cond_l[k] = before(cr, 0.0, axis)
        v = volts_in[layer[k]]
        put(VOLTS, k, [last(v, axis), last(cr, axis)], [first(v, axis)])
        if k == half - 1:
            pl.semaphore_wait(barrier, n_x + n_y - 2)
            start(VOLTS, 0)
    start(VOLTS, 1)

    for move in moves[2:6]:
        move.wait()
    pads = pad_conductance * pad_in[...].astype(jnp.float32)
    load = load_in[...]
    for k in range(layers):
        axis = axis_of(k)
        l = layer[k]
        up = jnp.minimum(l, layers - 2)
        va = via_in[up] * vmask_in[up].astype(jnp.float32) * jnp.where(l < layers - 1, 1.0, 0.0)
        vb = via_in[below[k]] * vmask_in[below[k]].astype(jnp.float32) * jnp.where(l > 0, 1.0, 0.0)
        top = pads * jnp.where(l == layers - 1, 1.0, 0.0)
        src = top * supply_volts - load * jnp.where(l == 0, 1.0, 0.0)
        via_a[k] = va
        via_b[k] = vb
        source[k] = src
        v = volts_in[l]
        cl, cr = cond_l[k], cond_r[k]
        dg = cl + cr + va + vb + top
        num = cl * before(v, 0.0, axis) + cr * after(v, 0.0, axis) + vb * volts_in[below[k]] + va * volts_in[above[k]] + src
        diag[k] = dg
        partial[k] = num
        put(PARTIAL, k, [last(num, axis), last(dg, axis)], [first(num, axis), first(dg, axis)])
        if k == half - 1:
            start(PARTIAL, 0)
    start(PARTIAL, 1)

    for move in moves[6:9]:
        move.wait()
    for k in range(layers):
        axis = axis_of(k)
        l = layer[k]
        mr = jnp.where(outer[axis], 0.0, mob_in[l] * (1.0 - blk_in[l].astype(jnp.float32)))
        mob_r[k] = mr
        s = stress_in[l]
        put(STRESS, k, [last(s, axis), last(mr, axis)], [first(s, axis)])
        if k == half - 1:
            start(STRESS, 0)
    start(STRESS, 1)

    def edge_next(k, v_prev, n_prev, v_next, n_next, v):
        axis = axis_of(k)
        c_in, c_out = halo(VOLTS, k, 0, 1), last(cond_r[k], axis)
        h_prev = (1.0 - damping) * v_prev + damping * (n_prev + c_in * first(v, axis)) / halo(PARTIAL, k, 0, 1)
        h_next = (1.0 - damping) * v_next + damping * (n_next + c_out * last(v, axis)) / (halo(PARTIAL, k, 1, 1) + c_out)
        return h_prev, h_next

    arrive(VOLTS)
    for k in range(layers):
        axis = axis_of(k)
        c_in = halo(VOLTS, k, 0, 1)
        cl = jnp.where(is_first[axis], c_in, cond_l[k])
        cond_l[k] = cl
        dg = diag[k] + jnp.where(is_first[axis], c_in, 0.0)
        diag[k] = dg
        w = damping / dg
        weight[k] = w
        num = partial[k] + jnp.where(is_first[axis], c_in * halo(VOLTS, k, 0, 0), 0.0)
        num = num + jnp.where(is_last[axis], cond_r[k] * halo(VOLTS, k, 1, 0), 0.0)
        volts_a[k] = (1.0 - damping) * volts_in[layer[k]] + w * num

    def inflow(v_ref, k, v, h_prev, h_next):
        axis = axis_of(k)
        lateral = cond_l[k] * before(v, h_prev, axis) + cond_r[k] * after(v, h_next, axis)
        return lateral + via_b[k] * v_ref[slot_below[k]] + via_a[k] * v_ref[slot_above[k]] + source[k]

    arrive(PARTIAL)
    for k in range(layers):
        v = volts_a[k]
        h_prev, h_next = edge_next(
            k, halo(VOLTS, k, 0, 0), halo(PARTIAL, k, 0, 0), halo(VOLTS, k, 1, 0), halo(PARTIAL, k, 1, 0),
            volts_in[layer[k]],
        )
        volts_b[k] = (1.0 - damping) * v + weight[k] * inflow(volts_a, k, v, h_prev, h_next)
    for k in range(layers):
        axis = axis_of(k)
        v = volts_b[k]
        num = inflow(volts_b, k, v, 0.0, 0.0)
        partial[k] = num
        put(VOLTS2, k, [last(v, axis), last(num, axis)], [first(v, axis), first(num, axis)])
        if k == half - 1:
            start(VOLTS2, 0)
    start(VOLTS2, 1)

    arrive(STRESS)
    for k in range(layers):
        axis = axis_of(k)
        mr = mob_r[k]
        ml = before(mr, halo(STRESS, k, 0, 1), axis)
        mob_l[k] = ml
        wind_r[k] = wind_factor * mr * cond_r[k]
        wind_l[k] = wind_factor * ml * cond_l[k]

    arrive(VOLTS2)
    for k in range(layers):
        axis = axis_of(k)
        num = partial[k] + jnp.where(is_first[axis], cond_l[k] * halo(VOLTS2, k, 0, 0), 0.0)
        num = num + jnp.where(is_last[axis], cond_r[k] * halo(VOLTS2, k, 1, 0), 0.0)
        volts_a[k] = (1.0 - damping) * volts_b[k] + weight[k] * num

    total = jnp.zeros(shape, jnp.float32)
    for k in range(layers):
        axis = axis_of(k)
        v = volts_a[k]
        h_prev, h_next = edge_next(
            k, halo(VOLTS2, k, 0, 0), halo(VOLTS2, k, 0, 1), halo(VOLTS2, k, 1, 0), halo(VOLTS2, k, 1, 1), volts_b[k]
        )
        v_prev, v_next = before(v, h_prev, axis), after(v, h_next, axis)
        resid = cond_l[k] * v_prev + cond_r[k] * v_next + via_b[k] * volts_a[slot_below[k]]
        resid = resid + via_a[k] * volts_a[slot_above[k]] + source[k] - diag[k] * v
        total = total + resid * resid
        drift = wind_r[k] * (v - v_next) - wind_l[k] * (v_prev - v)
        mr, ml = mob_r[k], mob_l[k]
        s = stress_in[layer[k]]
        s_prev, s_next = before(s, halo(STRESS, k, 0, 0), axis), after(s, halo(STRESS, k, 1, 0), axis)
        s = s + mr * (s_next - s) - ml * (s - s_prev) + drift
        stress_a[k] = s
        part = s + mr * (after(s, 0.0, axis) - s) - ml * (s - before(s, 0.0, axis)) + drift
        partial[k] = part
        weight[k] = drift
        put(STRESS1, k, [last(s, axis), last(part, axis)], [first(s, axis), first(part, axis)])
        if k == half - 1:
            start(STRESS1, 0)
    start(STRESS1, 1)

    def sum_copy(group, sem_s, sem_r, o, axis, sender):
        me, n = (gx, n_x) if axis == 0 else (gy, n_y)
        other = lax.rem(me + o, n)
        slot = me if sender else other
        return pltpu.make_async_remote_copy(
            src_ref=group.at[me], dst_ref=group.at[slot], send_sem=sem_s.at[o - 1], recv_sem=sem_r.at[slot],
            device_id=(other, gy) if axis == 0 else (gx, other), device_id_type=MESH,
        )

    def fold(a):
        r = a[0:8]
        for i in range(8, a.shape[0], 8):
            r = r + a[i:i + 8]
        out = r[:, 0:128]
        for j in range(128, a.shape[1], 128):
            out = out + r[:, j:j + 128]
        return out

    sum_x[gx] = fold(total)
    for o in range(1, n_x):
        sum_copy(sum_x, sx_send, sx_recv, o, 0, True).start()

    for l in range(layers):
        volts_fin[l] = volts_a[pos[l]]
    out_v = pltpu.make_async_copy(volts_fin, volts_out, out_sem.at[0])
    out_v.start()

    for o in range(1, n_x):
        sum_copy(sum_x, sx_send, sx_recv, o, 0, False).wait_recv()
    along = sum_x[0]
    for i in range(1, n_x):
        along = along + sum_x[i]
    sum_y[gy] = along
    for o in range(1, n_y):
        sum_copy(sum_y, sy_send, sy_recv, o, 1, True).start()

    arrive(STRESS1)
    for k in range(layers):
        axis = axis_of(k)
        mr, ml, s1 = mob_r[k], mob_l[k], stress_a[k]
        m_in, m_out = first(ml, axis), last(mr, axis)
        s_prev, s_next = halo(STRESS1, k, 0, 0), halo(STRESS1, k, 1, 0)
        s = partial[k] + jnp.where(is_first[axis], ml * s_prev, 0.0) + jnp.where(is_last[axis], mr * s_next, 0.0)
        h_prev = halo(STRESS1, k, 0, 1) + m_in * first(s1, axis)
        h_next = halo(STRESS1, k, 1, 1) + m_out * last(s1, axis)
        s = s + mr * (after(s, h_next, axis) - s) - ml * (s - before(s, h_prev, axis)) + weight[k]
        stress_a[k] = s
    for l in range(layers):
        stress_fin[l] = stress_a[pos[l]]
    out_s = pltpu.make_async_copy(stress_fin, stress_out, out_sem.at[1])
    out_s.start()

    for o in range(1, n_y):
        sum_copy(sum_y, sy_send, sy_recv, o, 1, False).wait_recv()
    whole = sum_y[0]
    for i in range(1, n_y):
        whole = whole + sum_y[i]
    nodes = layers * n_x * rows_x * n_y * rows_y
    mean = jnp.sum(whole, keepdims=True) * (1.0 / nodes)
    rms_out[0, 0] = jnp.sqrt(mean)[0, 0]

    for r in range(ROUNDS):
        for d in range(4):
            @pl.when(to_has[d])
            def _():
                edge_copy(r, d).wait_send()
    for o in range(1, n_x):
        sum_copy(sum_x, sx_send, sx_recv, o, 0, True).wait_send()
    for o in range(1, n_y):
        sum_copy(sum_y, sy_send, sy_recv, o, 1, True).wait_send()
    out_v.wait()
    out_s.wait()


def body(n_x, n_y, volts_start, seg_cond, via_cond, via_mask, pad_mask, load_current, stress_start, mobility, blocked, layer_dirs):
    layers, rows_x, rows_y = seg_cond.shape
    half = layers // 2
    f32, i32 = jnp.float32, jnp.int32
    full = (layers, rows_x, rows_y)
    vias = via_cond.shape
    flat = (rows_x, rows_y)
    dma = pltpu.SemaphoreType.DMA
    out = pl.BlockSpec(memory_space=pl.ANY)
    hbm = pl.BlockSpec(memory_space=pltpu.HBM)
    operands = (
        layer_dirs, volts_start, seg_cond, via_cond, via_mask, pad_mask, load_current, stress_start, mobility, blocked
    )
    volts, stress, rms = pl.pallas_call(
        functools.partial(kernel, n_x, n_y, layers, rows_x, rows_y),
        out_shape=(
            jax.ShapeDtypeStruct(full, f32),
            jax.ShapeDtypeStruct(full, f32),
            jax.ShapeDtypeStruct((1, 1), f32),
        ),
        in_specs=[hbm] * 10,
        out_specs=(out, out, pl.BlockSpec(memory_space=pltpu.SMEM)),
        scratch_shapes=[
            pltpu.SMEM((layers,), i32),
            pltpu.VMEM(full, f32), pltpu.VMEM(full, f32), pltpu.VMEM(vias, f32), pltpu.VMEM(vias, i32),
            pltpu.VMEM(flat, i32), pltpu.VMEM(flat, f32), pltpu.VMEM(full, f32), pltpu.VMEM(full, f32), pltpu.VMEM(full, i32),
        ]
        + [pltpu.VMEM(full, f32)] * 17
        + [
            pltpu.VMEM((ROUNDS, 2, 2, half, rows_y), f32), pltpu.VMEM((ROUNDS, 2, 2, half, rows_y), f32),
            pltpu.VMEM((ROUNDS, 2, half, rows_x, 128), f32), pltpu.VMEM((ROUNDS, 2, half, rows_x, 128), f32),
            pltpu.VMEM((n_x, 8, 128), f32), pltpu.VMEM((n_y, 8, 128), f32),
            dma((10,)), dma((2,)), dma((ROUNDS, 4)), dma((ROUNDS, 4)),
            dma((n_x,)), dma((n_x,)), dma((n_y,)), dma((n_y,)),
        ],
        compiler_params=pltpu.CompilerParams(
            collective_id=0, has_side_effects=True, vmem_limit_bytes=40 * 1024 * 1024
        ),
        cost_estimate=pl.CostEstimate(flops=20_000_000, bytes_accessed=5_000_000, transcendentals=0),
    )(*[pltpu.with_memory_space_constraint(operand, pltpu.HBM) for operand in operands])
    return volts, stress, rms.reshape(())


def solution(mesh):
    tile = P(None, "gx", "gy")
    flat = P("gx", "gy")
    in_specs = (tile, tile, tile, tile, flat, flat, tile, tile, tile, P())
    return jax.shard_map(
        functools.partial(body, mesh.shape["gx"], mesh.shape["gy"]),
        mesh=mesh, in_specs=in_specs, out_specs=(tile, tile, P()), check_vma=False,
    )
```

```python
import functools
import jax
import jax.numpy as jnp
from jax import lax
from jax.experimental import pallas as pl
from jax.experimental.pallas import tpu as pltpu
from jax.sharding import PartitionSpec as P

damping = 0.8
pad_conductance = 4.0
supply_volts = 1.0
wind_factor = 4.0

MESH = pl.DeviceIdType.MESH
VOLTS, STRESS, PARTIAL, VOLTS2, STRESS1 = range(5)
ROUNDS = 5


def kernel(
    n_x, n_y, layers, rows_x, rows_y,
    dirs_hbm, volts_hbm, seg_hbm, via_hbm, vmask_hbm, pad_hbm, load_hbm, stress_hbm, mob_hbm, blk_hbm,
    volts_out, stress_out, rms_out,
    dirs, volts_in, seg_in, via_in, vmask_in, pad_in, load_in, stress_in, mob_in, blk_in,
    cond, via_b, via_a, source, anchor, diag, weight, partial, mob, volts_a, volts_b, stress_a, stress_b,
    volts_fin, stress_fin,
    send_x, recv_x, send_y, recv_y, sum_x, sum_y,
    in_sem, out_sem, send_sem, recv_sem, sx_send, sx_recv, sy_send, sy_recv,
):
    half = layers // 2
    gx = lax.axis_index("gx")
    gy = lax.axis_index("gy")

    moves = [
        pltpu.make_async_copy(src, dst, in_sem.at[i])
        for i, (src, dst) in enumerate(
            [
                (volts_hbm, volts_in), (seg_hbm, seg_in), (via_hbm, via_in), (vmask_hbm, vmask_in), (pad_hbm, pad_in),
                (load_hbm, load_in), (stress_hbm, stress_in), (mob_hbm, mob_in), (blk_hbm, blk_in), (dirs_hbm, dirs),
            ]
        )
    ]
    moves[9].start()
    for move in moves[:9]:
        move.start()

    barrier = pltpu.get_barrier_semaphore()
    for o in range(1, n_x):
        pl.semaphore_signal(barrier, inc=1, device_id=(lax.rem(gx + o, n_x), gy), device_id_type=MESH)
    for o in range(1, n_y):
        pl.semaphore_signal(barrier, inc=1, device_id=(gx, lax.rem(gy + o, n_y)), device_id_type=MESH)

    to_has = [gx < n_x - 1, gx > 0, gy < n_y - 1, gy > 0]
    from_has = [gx > 0, gx < n_x - 1, gy > 0, gy < n_y - 1]
    target = [
        (jnp.minimum(gx + 1, n_x - 1), gy), (jnp.maximum(gx - 1, 0), gy),
        (gx, jnp.minimum(gy + 1, n_y - 1)), (gx, jnp.maximum(gy - 1, 0)),
    ]

    def edge_copy(r, d):
        if d < 2:
            count = 1 if (d == 1 and r in (VOLTS, STRESS)) else 2
            src, dst = send_x.at[r, d, 0:count], recv_x.at[r, d, 0:count]
        else:
            src, dst = send_y.at[r, d - 2], recv_y.at[r, d - 2]
        return pltpu.make_async_remote_copy(
            src_ref=src, dst_ref=dst, send_sem=send_sem.at[r, d], recv_sem=recv_sem.at[r, d],
            device_id=target[d], device_id_type=MESH,
        )

    def start(r, axis):
        for d in (2 * axis, 2 * axis + 1):
            @pl.when(to_has[d])
            def _():
                edge_copy(r, d).start()

    def arrive(r):
        for d in range(4):
            @pl.when(from_has[d])
            def _():
                edge_copy(r, d).wait_recv()

    for d in range(2):
        @pl.when(jnp.logical_not(from_has[d]))
        def _():
            for r in range(ROUNDS):
                recv_x[r, d] = jnp.full(recv_x.shape[2:], 1.0 if r == PARTIAL else 0.0, jnp.float32)

        @pl.when(jnp.logical_not(from_has[d + 2]))
        def _():
            for r in range(ROUNDS):
                recv_y[r, d] = jnp.full(recv_y.shape[2:], 1.0 if r == PARTIAL else 0.0, jnp.float32)

    moves[9].wait()
    is_y = [dirs[l] for l in range(layers)]
    pos = []
    seen_x, seen_y = jnp.int32(0), jnp.int32(half)
    for l in range(layers):
        pos.append(jnp.where(is_y[l] == 1, seen_y, seen_x))
        seen_y = seen_y + is_y[l]
        seen_x = seen_x + 1 - is_y[l]
    layer = []
    for k in range(layers):
        at = jnp.int32(0)
        for l in range(1, layers):
            at = at + jnp.where(pos[l] == k, l, 0)
        layer.append(at)

    def slot_of(want):
        at = jnp.int32(0)
        for k in range(1, layers):
            at = at + jnp.where(layer[k] == want, k, 0)
        return at

    below = [jnp.maximum(layer[k] - 1, 0) for k in range(layers)]
    above = [jnp.minimum(layer[k] + 1, layers - 1) for k in range(layers)]
    slot_below = [slot_of(below[k]) for k in range(layers)]
    slot_above = [slot_of(above[k]) for k in range(layers)]

    shape = (rows_x, rows_y)
    index = [lax.broadcasted_iota(jnp.int32, shape, 0), lax.broadcasted_iota(jnp.int32, shape, 1)]
    length = [rows_x, rows_y]
    is_first = [index[0] == 0, index[1] == 0]
    is_last = [index[0] == rows_x - 1, index[1] == rows_y - 1]
    outer = [
        jnp.logical_and(is_last[0], gx == n_x - 1),
        jnp.logical_and(is_last[1], gy == n_y - 1),
    ]
    lane = lax.broadcasted_iota(jnp.int32, (rows_x, 128), 1)

    def axis_of(k):
        return 0 if k < half else 1

    def before(a, h, axis):
        return jnp.where(is_first[axis], h, pltpu.roll(a, 1, axis))

    def after(a, h, axis):
        return jnp.where(is_last[axis], h, pltpu.roll(a, length[axis] - 1, axis))

    def first(a, axis):
        return a[0:1, :] if axis == 0 else a[:, 0:1]

    def last(a, axis):
        return a[rows_x - 1:rows_x, :] if axis == 0 else a[:, rows_y - 1:rows_y]

    def put(r, k, to_next, to_prev):
        for d, values in ((0, to_next), (1, to_prev)):
            if k < half:
                for i, value in enumerate(values):
                    send_x[r, d, i, k:k + 1, :] = value
            else:
                packed = jnp.broadcast_to(values[0], (rows_x, 128))
                if len(values) > 1:
                    packed = jnp.where(lane == 0, packed, values[1])
                send_y[r, d, k - half] = packed

    def halo(r, k, d, i):
        if k < half:
            return recv_x[r, d, i, k:k + 1, :]
        return recv_y[r, d, k - half, :, i:i + 1]

    moves[0].wait()
    moves[1].wait()
    for k in range(layers):
        axis = axis_of(k)
        cr = jnp.where(outer[axis], 0.0, seg_in[layer[k]])
        cond[k] = cr
        v = volts_in[layer[k]]
        put(VOLTS, k, [last(v, axis), last(cr, axis)], [first(v, axis)])
        if k == half - 1:
            pl.semaphore_wait(barrier, n_x + n_y - 2)
            start(VOLTS, 0)
    start(VOLTS, 1)

    def inside(k, coef, field, minus=None):
        axis = axis_of(k)
        flux = coef * (pltpu.roll(field, length[axis] - 1, axis) - field)
        if minus is not None:
            flux = flux - minus
        flux = jnp.where(is_last[axis], 0.0, flux)
        return flux - pltpu.roll(flux, 1, axis)

    def upright(k, v, v_below, v_above):
        return via_b[k] * v_below + via_a[k] * v_above + source[k] - anchor[k] * v

    for move in moves[2:6]:
        move.wait()
    pads = pad_conductance * pad_in[...].astype(jnp.float32)
    load = load_in[...]
    for k in range(layers):
        axis = axis_of(k)
        l = layer[k]
        up = jnp.minimum(l, layers - 2)
        va = via_in[up] * (vmask_in[up].astype(jnp.float32) * jnp.where(l < layers - 1, 1.0, 0.0))
        vb = via_in[below[k]] * (vmask_in[below[k]].astype(jnp.float32) * jnp.where(l > 0, 1.0, 0.0))
        top = pads * jnp.where(l == layers - 1, 1.0, 0.0)
        src = top * supply_volts - load * jnp.where(l == 0, 1.0, 0.0)
        hold = va + vb + top
        via_a[k] = va
        via_b[k] = vb
        source[k] = src
        anchor[k] = hold
        v = volts_in[l]
        cr = cond[k]
        dg = hold + cr + before(cr, 0.0, axis)
        res = inside(k, cr, v) + vb * volts_in[below[k]] + va * volts_in[above[k]] + src - hold * v
        diag[k] = dg
        partial[k] = res
        put(PARTIAL, k, [last(res, axis), last(dg, axis)], [first(res, axis), first(dg, axis)])
        if k == half - 1:
            start(PARTIAL, 0)
    start(PARTIAL, 1)

    for move in moves[6:9]:
        move.wait()
    for k in range(layers):
        axis = axis_of(k)
        l = layer[k]
        mr = jnp.where(outer[axis], 0.0, mob_in[l] * (1.0 - blk_in[l].astype(jnp.float32)))
        mob[k] = mr
        s = stress_in[l]
        put(STRESS, k, [last(s, axis), last(mr, axis)], [first(s, axis)])
        if k == half - 1:
            start(STRESS, 0)
    start(STRESS, 1)

    def edge_next(k, v_prev, r_prev, v_next, r_next, v):
        axis = axis_of(k)
        c_in, c_out = halo(VOLTS, k, 0, 1), last(cond[k], axis)
        h_prev = v_prev + damping * (r_prev + c_in * (first(v, axis) - v_prev)) / halo(PARTIAL, k, 0, 1)
        h_next = v_next + damping * (r_next + c_out * (last(v, axis) - v_next)) / (halo(PARTIAL, k, 1, 1) + c_out)
        return h_prev, h_next

    def edges(axis, at_first, at_last):
        return jnp.where(is_first[axis], at_first, jnp.where(is_last[axis], at_last, 0.0))

    arrive(VOLTS)
    for k in range(layers):
        axis = axis_of(k)
        c_in, c_out = halo(VOLTS, k, 0, 1), last(cond[k], axis)
        v = volts_in[layer[k]]
        w = damping / (diag[k] + jnp.where(is_first[axis], c_in, 0.0))
        weight[k] = w
        cross = edges(
            axis, c_in * (halo(VOLTS, k, 0, 0) - first(v, axis)), c_out * (halo(VOLTS, k, 1, 0) - last(v, axis))
        )
        volts_a[k] = v + w * (partial[k] + cross)

    arrive(PARTIAL)
    for k in range(layers):
        axis = axis_of(k)
        v = volts_a[k]
        h_prev, h_next = edge_next(
            k, halo(VOLTS, k, 0, 0), halo(PARTIAL, k, 0, 0), halo(VOLTS, k, 1, 0), halo(PARTIAL, k, 1, 0),
            volts_in[layer[k]],
        )
        flux = cond[k] * (after(v, h_next, axis) - v)
        net = flux - before(flux, halo(VOLTS, k, 0, 1) * (first(v, axis) - h_prev), axis)
        volts_b[k] = v + weight[k] * (net + upright(k, v, volts_a[slot_below[k]], volts_a[slot_above[k]]))
    for k in range(layers):
        axis = axis_of(k)
        v = volts_b[k]
        res = inside(k, cond[k], v) + upright(k, v, volts_b[slot_below[k]], volts_b[slot_above[k]])
        volts_a[k] = v + weight[k] * res
        put(VOLTS2, k, [last(v, axis), last(res, axis)], [first(v, axis), first(res, axis)])
        if k == half - 1:
            start(VOLTS2, 0)
    start(VOLTS2, 1)

    arrive(STRESS)
    for k in range(layers):
        axis = axis_of(k)
        s = stress_in[layer[k]]
        flux = mob[k] * (after(s, halo(STRESS, k, 1, 0), axis) - s)
        at_first = halo(STRESS, k, 0, 1) * (first(s, axis) - halo(STRESS, k, 0, 0))
        stress_a[k] = s + flux - before(flux, at_first, axis)

    arrive(VOLTS2)
    entry, pull = [], []
    for k in range(layers):
        axis = axis_of(k)
        c_in, c_out = halo(VOLTS, k, 0, 1), last(cond[k], axis)
        v_prev, v_next, v = halo(VOLTS2, k, 0, 0), halo(VOLTS2, k, 1, 0), volts_b[k]
        h_prev, h_next = edge_next(k, v_prev, halo(VOLTS2, k, 0, 1), v_next, halo(VOLTS2, k, 1, 1), v)
        cross = edges(axis, c_in * (v_prev - first(v, axis)), c_out * (v_next - last(v, axis)))
        v = volts_a[k] + weight[k] * cross
        volts_a[k] = v
        flux = cond[k] * (after(v, h_next, axis) - v)
        partial[k] = flux
        at_first = c_in * (first(v, axis) - h_prev)
        mr = mob[k]
        wind = wind_factor * mr * flux
        diag[k] = wind
        wind_first = wind_factor * halo(STRESS, k, 0, 1) * at_first
        entry.append(at_first)
        pull.append(wind_first)
        s = stress_a[k] - wind + before(wind, wind_first, axis)
        stress_a[k] = s
        part = s + inside(k, mr, s, wind)
        stress_b[k] = part
        put(STRESS1, k, [last(s, axis), last(part, axis)], [first(s, axis), first(part, axis)])
        if k == half - 1:
            start(STRESS1, 0)
    start(STRESS1, 1)

    total = jnp.zeros(shape, jnp.float32)
    for k in range(layers):
        flux = partial[k]
        net = flux - before(flux, entry[k], axis_of(k))
        res = net + upright(k, volts_a[k], volts_a[slot_below[k]], volts_a[slot_above[k]])
        total = total + res * res

    def sum_copy(group, sem_s, sem_r, o, axis, sender):
        me, n = (gx, n_x) if axis == 0 else (gy, n_y)
        other = lax.rem(me + o, n)
        slot = me if sender else other
        return pltpu.make_async_remote_copy(
            src_ref=group.at[me], dst_ref=group.at[slot], send_sem=sem_s.at[o - 1], recv_sem=sem_r.at[slot],
            device_id=(other, gy) if axis == 0 else (gx, other), device_id_type=MESH,
        )

    def fold(a):
        r = a[0:8]
        for i in range(8, a.shape[0], 8):
            r = r + a[i:i + 8]
        out = r[:, 0:128]
        for j in range(128, a.shape[1], 128):
            out = out + r[:, j:j + 128]
        return out

    sum_x[gx] = fold(total)
    for o in range(1, n_x):
        sum_copy(sum_x, sx_send, sx_recv, o, 0, True).start()

    for l in range(layers):
        volts_fin[l] = volts_a[pos[l]]
    out_v = pltpu.make_async_copy(volts_fin, volts_out, out_sem.at[0])
    out_v.start()

    arrive(STRESS1)
    for k in range(layers):
        axis = axis_of(k)
        mr, wind, s = mob[k], diag[k], stress_a[k]
        m_in, m_out = halo(STRESS, k, 0, 1), last(mr, axis)
        s_prev, s_next = halo(STRESS1, k, 0, 0), halo(STRESS1, k, 1, 0)
        flux_in = m_in * (first(s, axis) - s_prev) - pull[k]
        flux_out = m_out * (s_next - last(s, axis)) - last(wind, axis)
        s = stress_b[k] + edges(axis, -flux_in, flux_out)
        h_prev = halo(STRESS1, k, 0, 1) + flux_in
        h_next = halo(STRESS1, k, 1, 1) - flux_out
        flux = mr * (after(s, h_next, axis) - s) - wind
        stress_a[k] = s + flux - before(flux, m_in * (first(s, axis) - h_prev) - pull[k], axis)
        if k == half - 1:
            for o in range(1, n_x):
                sum_copy(sum_x, sx_send, sx_recv, o, 0, False).wait_recv()
            along = sum_x[0]
            for i in range(1, n_x):
                along = along + sum_x[i]
            sum_y[gy] = along
            for o in range(1, n_y):
                sum_copy(sum_y, sy_send, sy_recv, o, 1, True).start()
    for l in range(layers):
        stress_fin[l] = stress_a[pos[l]]
    out_s = pltpu.make_async_copy(stress_fin, stress_out, out_sem.at[1])
    out_s.start()

    for o in range(1, n_y):
        sum_copy(sum_y, sy_send, sy_recv, o, 1, False).wait_recv()
    whole = sum_y[0]
    for i in range(1, n_y):
        whole = whole + sum_y[i]
    nodes = layers * n_x * rows_x * n_y * rows_y
    mean = jnp.sum(whole, keepdims=True) * (1.0 / nodes)
    rms_out[0, 0] = jnp.sqrt(mean)[0, 0]

    for r in range(ROUNDS):
        for d in range(4):
            @pl.when(to_has[d])
            def _():
                edge_copy(r, d).wait_send()
    for o in range(1, n_x):
        sum_copy(sum_x, sx_send, sx_recv, o, 0, True).wait_send()
    for o in range(1, n_y):
        sum_copy(sum_y, sy_send, sy_recv, o, 1, True).wait_send()
    out_v.wait()
    out_s.wait()


def deliver(volts_ref, stress_ref, volts_out, stress_out, sems):
    parts = sems.shape[1]
    count = volts_ref.shape[0] // parts
    moves = [
        pltpu.make_async_copy(src.at[i * count:(i + 1) * count], dst.at[i * count:(i + 1) * count], sems.at[j, i])
        for j, (src, dst) in enumerate([(volts_ref, volts_out), (stress_ref, stress_out)])
        for i in range(parts)
    ]
    for move in moves:
        move.start()
    for move in moves:
        move.wait()


def body(n_x, n_y, volts_start, seg_cond, via_cond, via_mask, pad_mask, load_current, stress_start, mobility, blocked, layer_dirs):
    layers, rows_x, rows_y = seg_cond.shape
    half = layers // 2
    f32, i32 = jnp.float32, jnp.int32
    full = (layers, rows_x, rows_y)
    vias = via_cond.shape
    flat = (rows_x, rows_y)
    dma = pltpu.SemaphoreType.DMA
    out = pl.BlockSpec(memory_space=pl.ANY)
    hbm = pl.BlockSpec(memory_space=pltpu.HBM)
    operands = (
        layer_dirs, volts_start, seg_cond, via_cond, via_mask, pad_mask, load_current, stress_start, mobility, blocked
    )
    volts, stress, rms = pl.pallas_call(
        functools.partial(kernel, n_x, n_y, layers, rows_x, rows_y),
        out_shape=(
            jax.ShapeDtypeStruct(full, f32),
            jax.ShapeDtypeStruct(full, f32),
            jax.ShapeDtypeStruct((1, 1), f32),
        ),
        in_specs=[hbm] * 10,
        out_specs=(out, out, pl.BlockSpec(memory_space=pltpu.SMEM)),
        scratch_shapes=[
            pltpu.SMEM((layers,), i32),
            pltpu.VMEM(full, f32), pltpu.VMEM(full, f32), pltpu.VMEM(vias, f32), pltpu.VMEM(vias, i32),
            pltpu.VMEM(flat, i32), pltpu.VMEM(flat, f32), pltpu.VMEM(full, f32), pltpu.VMEM(full, f32), pltpu.VMEM(full, i32),
        ]
        + [pltpu.VMEM(full, f32)] * 15
        + [
            pltpu.VMEM((ROUNDS, 2, 2, half, rows_y), f32), pltpu.VMEM((ROUNDS, 2, 2, half, rows_y), f32),
            pltpu.VMEM((ROUNDS, 2, half, rows_x, 128), f32), pltpu.VMEM((ROUNDS, 2, half, rows_x, 128), f32),
            pltpu.VMEM((n_x, 8, 128), f32), pltpu.VMEM((n_y, 8, 128), f32),
            dma((10,)), dma((2,)), dma((ROUNDS, 4)), dma((ROUNDS, 4)),
            dma((n_x,)), dma((n_x,)), dma((n_y,)), dma((n_y,)),
        ],
        compiler_params=pltpu.CompilerParams(
            collective_id=0, has_side_effects=True, vmem_limit_bytes=40 * 1024 * 1024
        ),
        cost_estimate=pl.CostEstimate(flops=20_000_000, bytes_accessed=5_000_000, transcendentals=0),
    )(*[pltpu.with_memory_space_constraint(operand, pltpu.HBM) for operand in operands])
    volts, stress = pl.pallas_call(
        deliver,
        out_shape=(jax.ShapeDtypeStruct(full, f32), jax.ShapeDtypeStruct(full, f32)),
        in_specs=[out, out],
        out_specs=(hbm, hbm),
        scratch_shapes=[dma((2, 4))],
        cost_estimate=pl.CostEstimate(flops=0, bytes_accessed=2_000_000, transcendentals=0),
    )(volts, stress)
    return volts, stress, rms.reshape(())


def solution(mesh):
    tile = P(None, "gx", "gy")
    flat = P("gx", "gy")
    in_specs = (tile, tile, tile, tile, flat, flat, tile, tile, tile, P())
    return jax.shard_map(
        functools.partial(body, mesh.shape["gx"], mesh.shape["gy"]),
        mesh=mesh, in_specs=in_specs, out_specs=(tile, tile, P()), check_vma=False,
    )
```

```python
import functools
import jax
import jax.numpy as jnp
from jax import lax
from jax.experimental import pallas as pl
from jax.experimental.pallas import tpu as pltpu
from jax.sharding import PartitionSpec as P

damping = 0.8
pad_conductance = 4.0
supply_volts = 1.0
wind_factor = 4.0

MESH = pl.DeviceIdType.MESH
VOLTS, STRESS, PARTIAL, VOLTS2, STRESS1 = range(5)
ROUNDS = 5


def kernel(
    n_x, n_y, n_a, n_b, layers, rows_x, rows_y,
    dirs_hbm, volts_hbm, seg_hbm, via_hbm, vmask_hbm, pad_hbm, load_hbm, stress_hbm, mob_hbm, blk_hbm,
    volts_out, stress_out, rms_out,
    dirs, volts_in, seg_in, via_in, vmask_in, pad_in, load_in, stress_in, mob_in, blk_in,
    cond, via_b, via_a, source, anchor, diag, weight, partial, mob, volts_a, volts_b, stress_a, stress_b,
    volts_fin, stress_fin,
    send_x, recv_x, send_y, recv_y, sum_a, sum_b,
    in_sem, out_sem, send_sem, recv_sem, sa_send, sa_recv, sb_send, sb_recv,
):
    half = layers // 2
    gx = lax.axis_index("gx")
    gy = lax.axis_index("gy")

    moves = [
        pltpu.make_async_copy(src, dst, in_sem.at[i])
        for i, (src, dst) in enumerate(
            [
                (volts_hbm, volts_in), (seg_hbm, seg_in), (via_hbm, via_in), (vmask_hbm, vmask_in), (pad_hbm, pad_in),
                (load_hbm, load_in), (stress_hbm, stress_in), (mob_hbm, mob_in), (blk_hbm, blk_in), (dirs_hbm, dirs),
            ]
        )
    ]
    moves[9].start()
    for move in moves[:9]:
        move.start()

    barrier = pltpu.get_barrier_semaphore()
    me_a, me_b = (gx, gy) if n_b > 1 else (gx * n_y + gy, 0)

    def member(leg, o):
        if leg == 1:
            return gx, lax.rem(gy + o, n_b)
        other = lax.rem(me_a + o, n_a)
        return (other, gy) if n_b > 1 else (other // n_y, lax.rem(other, n_y))

    for leg, n in ((0, n_a), (1, n_b)):
        for o in range(1, n):
            pl.semaphore_signal(barrier, inc=1, device_id=member(leg, o), device_id_type=MESH)

    to_has = [gx < n_x - 1, gx > 0, gy < n_y - 1, gy > 0]
    from_has = [gx > 0, gx < n_x - 1, gy > 0, gy < n_y - 1]
    target = [
        (jnp.minimum(gx + 1, n_x - 1), gy), (jnp.maximum(gx - 1, 0), gy),
        (gx, jnp.minimum(gy + 1, n_y - 1)), (gx, jnp.maximum(gy - 1, 0)),
    ]

    def edge_copy(r, d):
        if d < 2:
            count = 1 if (d == 1 and r in (VOLTS, STRESS)) else 2
            src, dst = send_x.at[r, d, 0:count], recv_x.at[r, d, 0:count]
        else:
            src, dst = send_y.at[r, d - 2], recv_y.at[r, d - 2]
        return pltpu.make_async_remote_copy(
            src_ref=src, dst_ref=dst, send_sem=send_sem.at[r, d], recv_sem=recv_sem.at[r, d],
            device_id=target[d], device_id_type=MESH,
        )

    def start(r, axis):
        if r == VOLTS and axis == 0:
            pl.semaphore_wait(barrier, n_a - 1 + n_b - 1)
        for d in (2 * axis, 2 * axis + 1):
            @pl.when(to_has[d])
            def _():
                edge_copy(r, d).start()

    def arrive(r):
        for d in range(4):
            @pl.when(from_has[d])
            def _():
                edge_copy(r, d).wait_recv()

    for d in range(2):
        @pl.when(jnp.logical_not(from_has[d]))
        def _():
            for r in range(ROUNDS):
                recv_x[r, d] = jnp.full(recv_x.shape[2:], 1.0 if r == PARTIAL else 0.0, jnp.float32)

        @pl.when(jnp.logical_not(from_has[d + 2]))
        def _():
            for r in range(ROUNDS):
                recv_y[r, d] = jnp.full(recv_y.shape[2:], 1.0 if r == PARTIAL else 0.0, jnp.float32)

    moves[9].wait()
    is_y = [dirs[l] for l in range(layers)]
    pos = []
    seen_x, seen_y = jnp.int32(0), jnp.int32(half)
    for l in range(layers):
        pos.append(jnp.where(is_y[l] == 1, seen_y, seen_x))
        seen_y = seen_y + is_y[l]
        seen_x = seen_x + 1 - is_y[l]
    layer = []
    for k in range(layers):
        at = jnp.int32(0)
        for l in range(1, layers):
            at = at + jnp.where(pos[l] == k, l, 0)
        layer.append(at)

    def slot_of(want):
        at = jnp.int32(0)
        for k in range(1, layers):
            at = at + jnp.where(layer[k] == want, k, 0)
        return at

    below = [jnp.maximum(layer[k] - 1, 0) for k in range(layers)]
    above = [jnp.minimum(layer[k] + 1, layers - 1) for k in range(layers)]
    slot_below = [slot_of(below[k]) for k in range(layers)]
    slot_above = [slot_of(above[k]) for k in range(layers)]

    wide = rows_y // 2 if rows_y % 256 == 0 else rows_y
    tall = 8 if rows_x % 8 == 0 else rows_x
    cuts = [
        [(slice(0, rows_x), slice(j, j + wide)) for j in range(0, rows_y, wide)],
        [(slice(i, i + tall), slice(0, rows_y)) for i in range(0, rows_x, tall)],
    ]
    shapes = [(rows_x, wide), (tall, rows_y)]
    length = [rows_x, rows_y]
    index = [lax.broadcasted_iota(jnp.int32, shapes[axis], axis) for axis in range(2)]
    is_first = [index[axis] == 0 for axis in range(2)]
    is_last = [index[axis] == length[axis] - 1 for axis in range(2)]
    outer = [
        jnp.logical_and(is_last[0], gx == n_x - 1),
        jnp.logical_and(is_last[1], gy == n_y - 1),
    ]
    lane = lax.broadcasted_iota(jnp.int32, (tall, 128), 1)

    def pieces(r=None):
        for k in range(layers):
            axis = 0 if k < half else 1
            for rows, cols in cuts[axis]:
                yield k, axis, (rows, cols)
            if r is not None and k == half - 1:
                start(r, 0)
        if r is not None:
            start(r, 1)

    def take(ref, k, p):
        return ref[k, p[0], p[1]]

    def keep(ref, k, p, value):
        ref[k, p[0], p[1]] = value

    def before(a, h, axis):
        return jnp.where(is_first[axis], h, pltpu.roll(a, 1, axis))

    def after(a, h, axis):
        return jnp.where(is_last[axis], h, pltpu.roll(a, length[axis] - 1, axis))

    def first(a, axis):
        return a[0:1, :] if axis == 0 else a[:, 0:1]

    def last(a, axis):
        return a[rows_x - 1:rows_x, :] if axis == 0 else a[:, rows_y - 1:rows_y]

    def put(r, k, p, to_next, to_prev):
        for d, values in ((0, to_next), (1, to_prev)):
            if k < half:
                for i, value in enumerate(values):
                    send_x[r, d, i, k:k + 1, p[1]] = value
            else:
                packed = jnp.broadcast_to(values[0], (tall, 128))
                if len(values) > 1:
                    packed = jnp.where(lane == 0, packed, values[1])
                send_y[r, d, k - half, p[0], :] = packed

    def halo(r, k, p, d, i):
        if k < half:
            return recv_x[r, d, i, k:k + 1, p[1]]
        return recv_y[r, d, k - half, p[0], i:i + 1]

    def fold(a):
        r = a[0:8]
        for i in range(8, a.shape[0], 8):
            r = r + a[i:i + 8]
        out = r[:, 0:128]
        for j in range(128, a.shape[1], 128):
            out = out + r[:, j:j + 128]
        return out

    def sum_copy(leg, o, sender):
        group, me, n, sems = ((sum_a, me_a, n_a, (sa_send, sa_recv)), (sum_b, me_b, n_b, (sb_send, sb_recv)))[leg]
        slot = me if sender else lax.rem(me + o, n)
        return pltpu.make_async_remote_copy(
            src_ref=group.at[me], dst_ref=group.at[slot], send_sem=sems[0].at[o - 1], recv_sem=sems[1].at[slot],
            device_id=member(leg, o), device_id_type=MESH,
        )

    def first_leg():
        for o in range(1, n_a):
            sum_copy(0, o, False).wait_recv()
        along = sum_a[0]
        for i in range(1, n_a):
            along = along + sum_a[i]
        sum_b[me_b] = along
        for o in range(1, n_b):
            sum_copy(1, o, True).start()

    moves[0].wait()
    moves[1].wait()
    for k, axis, p in pieces(VOLTS):
        cr = jnp.where(outer[axis], 0.0, take(seg_in, layer[k], p))
        keep(cond, k, p, cr)
        v = take(volts_in, layer[k], p)
        put(VOLTS, k, p, [last(v, axis), last(cr, axis)], [first(v, axis)])

    def inside(axis, coef, field, minus=None):
        flux = coef * (pltpu.roll(field, length[axis] - 1, axis) - field)
        if minus is not None:
            flux = flux - minus
        flux = jnp.where(is_last[axis], 0.0, flux)
        return flux - pltpu.roll(flux, 1, axis)

    def upright(k, p, v, v_below, v_above):
        return take(via_b, k, p) * v_below + take(via_a, k, p) * v_above + take(source, k, p) - take(anchor, k, p) * v

    for move in moves[2:6]:
        move.wait()
    for k, axis, p in pieces(PARTIAL):
        l = layer[k]
        up = jnp.minimum(l, layers - 2)
        va = take(via_in, up, p) * (take(vmask_in, up, p).astype(jnp.float32) * jnp.where(l < layers - 1, 1.0, 0.0))
        vb = take(via_in, below[k], p) * (take(vmask_in, below[k], p).astype(jnp.float32) * jnp.where(l > 0, 1.0, 0.0))
        pads = pad_conductance * pad_in[p[0], p[1]].astype(jnp.float32)
        top = pads * jnp.where(l == layers - 1, 1.0, 0.0)
        src = top * supply_volts - load_in[p[0], p[1]] * jnp.where(l == 0, 1.0, 0.0)
        hold = va + vb + top
        keep(via_a, k, p, va)
        keep(via_b, k, p, vb)
        keep(source, k, p, src)
        keep(anchor, k, p, hold)
        v = take(volts_in, l, p)
        cr = take(cond, k, p)
        dg = hold + cr + before(cr, 0.0, axis)
        res = inside(axis, cr, v) + vb * take(volts_in, below[k], p) + va * take(volts_in, above[k], p) + src - hold * v
        keep(diag, k, p, dg)
        keep(partial, k, p, res)
        put(PARTIAL, k, p, [last(res, axis), last(dg, axis)], [first(res, axis), first(dg, axis)])

    for move in moves[6:9]:
        move.wait()
    for k, axis, p in pieces(STRESS):
        l = layer[k]
        mr = jnp.where(outer[axis], 0.0, take(mob_in, l, p) * (1.0 - take(blk_in, l, p).astype(jnp.float32)))
        keep(mob, k, p, mr)
        s = take(stress_in, l, p)
        put(STRESS, k, p, [last(s, axis), last(mr, axis)], [first(s, axis)])

    def edge_next(k, p, v_prev, r_prev, v_next, r_next, v):
        axis = 0 if k < half else 1
        c_in, c_out = halo(VOLTS, k, p, 0, 1), last(take(cond, k, p), axis)
        h_prev = v_prev + damping * (r_prev + c_in * (first(v, axis) - v_prev)) / halo(PARTIAL, k, p, 0, 1)
        h_next = v_next + damping * (r_next + c_out * (last(v, axis) - v_next)) / (halo(PARTIAL, k, p, 1, 1) + c_out)
        return h_prev, h_next

    def edges(axis, at_first, at_last):
        return jnp.where(is_first[axis], at_first, jnp.where(is_last[axis], at_last, 0.0))

    arrive(VOLTS)
    for k, axis, p in pieces():
        c_in, c_out = halo(VOLTS, k, p, 0, 1), last(take(cond, k, p), axis)
        v = take(volts_in, layer[k], p)
        w = damping / (take(diag, k, p) + jnp.where(is_first[axis], c_in, 0.0))
        keep(weight, k, p, w)
        cross = edges(
            axis, c_in * (halo(VOLTS, k, p, 0, 0) - first(v, axis)), c_out * (halo(VOLTS, k, p, 1, 0) - last(v, axis))
        )
        keep(volts_a, k, p, v + w * (take(partial, k, p) + cross))

    arrive(PARTIAL)
    for k, axis, p in pieces():
        v = take(volts_a, k, p)
        h_prev, h_next = edge_next(
            k, p, halo(VOLTS, k, p, 0, 0), halo(PARTIAL, k, p, 0, 0), halo(VOLTS, k, p, 1, 0), halo(PARTIAL, k, p, 1, 0),
            take(volts_in, layer[k], p),
        )
        flux = take(cond, k, p) * (after(v, h_next, axis) - v)
        net = flux - before(flux, halo(VOLTS, k, p, 0, 1) * (first(v, axis) - h_prev), axis)
        keep(volts_b, k, p, v + take(weight, k, p) * (net + upright(k, p, v, take(volts_a, slot_below[k], p), take(volts_a, slot_above[k], p))))
    for k, axis, p in pieces(VOLTS2):
        v = take(volts_b, k, p)
        res = inside(axis, take(cond, k, p), v) + upright(k, p, v, take(volts_b, slot_below[k], p), take(volts_b, slot_above[k], p))
        keep(volts_a, k, p, v + take(weight, k, p) * res)
        put(VOLTS2, k, p, [last(v, axis), last(res, axis)], [first(v, axis), first(res, axis)])

    arrive(STRESS)
    for k, axis, p in pieces():
        s = take(stress_in, layer[k], p)
        flux = take(mob, k, p) * (after(s, halo(STRESS, k, p, 1, 0), axis) - s)
        at_first = halo(STRESS, k, p, 0, 1) * (first(s, axis) - halo(STRESS, k, p, 0, 0))
        keep(stress_a, k, p, s + flux - before(flux, at_first, axis))

    arrive(VOLTS2)
    entry, pull = [], []
    for k, axis, p in pieces(STRESS1):
        c_in, c_out = halo(VOLTS, k, p, 0, 1), last(take(cond, k, p), axis)
        v_prev, v_next, v = halo(VOLTS2, k, p, 0, 0), halo(VOLTS2, k, p, 1, 0), take(volts_b, k, p)
        h_prev, h_next = edge_next(k, p, v_prev, halo(VOLTS2, k, p, 0, 1), v_next, halo(VOLTS2, k, p, 1, 1), v)
        cross = edges(axis, c_in * (v_prev - first(v, axis)), c_out * (v_next - last(v, axis)))
        v = take(volts_a, k, p) + take(weight, k, p) * cross
        keep(volts_a, k, p, v)
        flux = take(cond, k, p) * (after(v, h_next, axis) - v)
        keep(partial, k, p, flux)
        at_first = c_in * (first(v, axis) - h_prev)
        mr = take(mob, k, p)
        wind = wind_factor * mr * flux
        keep(diag, k, p, wind)
        wind_first = wind_factor * halo(STRESS, k, p, 0, 1) * at_first
        entry.append(at_first)
        pull.append(wind_first)
        s = take(stress_a, k, p) - wind + before(wind, wind_first, axis)
        keep(stress_a, k, p, s)
        part = s + inside(axis, mr, s, wind)
        keep(stress_b, k, p, part)
        put(STRESS1, k, p, [last(s, axis), last(part, axis)], [first(s, axis), first(part, axis)])

    total = jnp.zeros((8, 128), jnp.float32)
    for i, (k, axis, p) in enumerate(pieces()):
        flux = take(partial, k, p)
        net = flux - before(flux, entry[i], axis)
        res = net + upright(k, p, take(volts_a, k, p), take(volts_a, slot_below[k], p), take(volts_a, slot_above[k], p))
        total = total + fold(res * res)

    sum_a[me_a] = jnp.sum(total, axis=0, keepdims=True)
    for o in range(1, n_a):
        sum_copy(0, o, True).start()

    for l in range(layers):
        volts_fin[l] = volts_a[pos[l]]
    out_v = pltpu.make_async_copy(volts_fin, volts_out, out_sem.at[0])
    out_v.start()

    arrive(STRESS1)
    for i, (k, axis, p) in enumerate(pieces()):
        mr, wind, s = take(mob, k, p), take(diag, k, p), take(stress_a, k, p)
        m_in, m_out = halo(STRESS, k, p, 0, 1), last(mr, axis)
        s_prev, s_next = halo(STRESS1, k, p, 0, 0), halo(STRESS1, k, p, 1, 0)
        flux_in = m_in * (first(s, axis) - s_prev) - pull[i]
        flux_out = m_out * (s_next - last(s, axis)) - last(wind, axis)
        s = take(stress_b, k, p) + edges(axis, -flux_in, flux_out)
        h_prev = halo(STRESS1, k, p, 0, 1) + flux_in
        h_next = halo(STRESS1, k, p, 1, 1) - flux_out
        flux = mr * (after(s, h_next, axis) - s) - wind
        keep(stress_a, k, p, s + flux - before(flux, m_in * (first(s, axis) - h_prev) - pull[i], axis))
        if n_b > 1 and k == half - 1 and p == cuts[0][-1]:
            first_leg()
    for l in range(layers):
        stress_fin[l] = stress_a[pos[l]]
    out_s = pltpu.make_async_copy(stress_fin, stress_out, out_sem.at[1])
    out_s.start()

    if n_b == 1:
        first_leg()
    for o in range(1, n_b):
        sum_copy(1, o, False).wait_recv()
    whole = sum_b[0]
    for i in range(1, n_b):
        whole = whole + sum_b[i]
    nodes = layers * n_x * rows_x * n_y * rows_y
    mean = jnp.sum(whole, keepdims=True) * (1.0 / nodes)
    rms_out[0, 0] = jnp.sqrt(mean)[0, 0]

    for r in range(ROUNDS):
        for d in range(4):
            @pl.when(to_has[d])
            def _():
                edge_copy(r, d).wait_send()
    for leg, n in ((0, n_a), (1, n_b)):
        for o in range(1, n):
            sum_copy(leg, o, True).wait_send()
    out_v.wait()
    out_s.wait()


def body(n_x, n_y, volts_start, seg_cond, via_cond, via_mask, pad_mask, load_current, stress_start, mobility, blocked, layer_dirs):
    layers, rows_x, rows_y = seg_cond.shape
    half = layers // 2
    n_a, n_b = (n_x * n_y, 1) if n_x * n_y <= 64 else (n_x, n_y)
    f32, i32 = jnp.float32, jnp.int32
    full = (layers, rows_x, rows_y)
    vias = via_cond.shape
    flat = (rows_x, rows_y)
    dma = pltpu.SemaphoreType.DMA
    out = pl.BlockSpec(memory_space=pl.ANY)
    hbm = pl.BlockSpec(memory_space=pltpu.HBM)
    operands = (
        layer_dirs, volts_start, seg_cond, via_cond, via_mask, pad_mask, load_current, stress_start, mobility, blocked
    )
    volts, stress, rms = pl.pallas_call(
        functools.partial(kernel, n_x, n_y, n_a, n_b, layers, rows_x, rows_y),
        out_shape=(
            jax.ShapeDtypeStruct(full, f32),
            jax.ShapeDtypeStruct(full, f32),
            jax.ShapeDtypeStruct((1, 1), f32),
        ),
        in_specs=[hbm] * 10,
        out_specs=(out, out, pl.BlockSpec(memory_space=pltpu.SMEM)),
        scratch_shapes=[
            pltpu.SMEM((layers,), i32),
            pltpu.VMEM(full, f32), pltpu.VMEM(full, f32), pltpu.VMEM(vias, f32), pltpu.VMEM(vias, i32),
            pltpu.VMEM(flat, i32), pltpu.VMEM(flat, f32), pltpu.VMEM(full, f32), pltpu.VMEM(full, f32), pltpu.VMEM(full, i32),
        ]
        + [pltpu.VMEM(full, f32)] * 15
        + [
            pltpu.VMEM((ROUNDS, 2, 2, half, rows_y), f32), pltpu.VMEM((ROUNDS, 2, 2, half, rows_y), f32),
            pltpu.VMEM((ROUNDS, 2, half, rows_x, 128), f32), pltpu.VMEM((ROUNDS, 2, half, rows_x, 128), f32),
            pltpu.VMEM((n_a, 1, 128), f32), pltpu.VMEM((n_b, 1, 128), f32),
            dma((10,)), dma((2,)), dma((ROUNDS, 4)), dma((ROUNDS, 4)),
            dma((n_a,)), dma((n_a,)), dma((n_b,)), dma((n_b,)),
        ],
        compiler_params=pltpu.CompilerParams(
            collective_id=0, has_side_effects=True, vmem_limit_bytes=40 * 1024 * 1024
        ),
        cost_estimate=pl.CostEstimate(flops=20_000_000, bytes_accessed=5_000_000, transcendentals=0),
    )(*[pltpu.with_memory_space_constraint(operand, pltpu.HBM) for operand in operands])
    return volts, stress, rms.reshape(())


def solution(mesh):
    tile = P(None, "gx", "gy")
    flat = P("gx", "gy")
    in_specs = (tile, tile, tile, tile, flat, flat, tile, tile, tile, P())
    return jax.shard_map(
        functools.partial(body, mesh.shape["gx"], mesh.shape["gy"]),
        mesh=mesh, in_specs=in_specs, out_specs=(tile, tile, P()), check_vma=False,
    )
```

```python
import functools
import jax
import jax.numpy as jnp
from jax import lax
from jax.experimental import pallas as pl
from jax.experimental.pallas import tpu as pltpu
from jax.sharding import PartitionSpec as P

damping = 0.8
pad_conductance = 4.0
supply_volts = 1.0
wind_factor = 4.0

MESH = pl.DeviceIdType.MESH
VOLTS, STRESS, PARTIAL, VOLTS2, STRESS1 = range(5)
ROUNDS = 5


def kernel(
    n_x, n_y, n_a, n_b, layers, rows_x, rows_y,
    dirs_hbm, volts_hbm, seg_hbm, via_hbm, vmask_hbm, pad_hbm, load_hbm, stress_hbm, mob_hbm, blk_hbm,
    volts_out, stress_out, rms_out,
    dirs, volts_in, seg_in, via_in, vmask_in, pad_in, load_in, stress_in, mob_in, blk_in,
    cond, via_b, via_a, source, anchor, diag, weight, partial, mob, volts_a, volts_b, stress_a, stress_b,
    volts_fin, stress_fin,
    send_x, recv_x, send_y, recv_y, sum_a, sum_b,
    in_sem, out_sem, send_sem, recv_sem, sa_send, sa_recv, sb_send, sb_recv,
):
    half = layers // 2
    gx = lax.axis_index("gx")
    gy = lax.axis_index("gy")

    moves = [
        pltpu.make_async_copy(src, dst, in_sem.at[i])
        for i, (src, dst) in enumerate(
            [
                (volts_hbm, volts_in), (seg_hbm, seg_in), (via_hbm, via_in), (vmask_hbm, vmask_in), (pad_hbm, pad_in),
                (load_hbm, load_in), (stress_hbm, stress_in), (mob_hbm, mob_in), (blk_hbm, blk_in), (dirs_hbm, dirs),
            ]
        )
    ]
    moves[9].start()
    for move in moves[:6]:
        move.start()

    barrier = pltpu.get_barrier_semaphore()
    me_a, me_b = (gx, gy) if n_b > 1 else (gx * n_y + gy, 0)

    def member(leg, o):
        if leg == 1:
            return gx, lax.rem(gy + o, n_b)
        other = lax.rem(me_a + o, n_a)
        return (other, gy) if n_b > 1 else (other // n_y, lax.rem(other, n_y))

    for leg, n in ((0, n_a), (1, n_b)):
        for o in range(1, n):
            pl.semaphore_signal(barrier, inc=1, device_id=member(leg, o), device_id_type=MESH)

    to_has = [gx < n_x - 1, gx > 0, gy < n_y - 1, gy > 0]
    from_has = [gx > 0, gx < n_x - 1, gy > 0, gy < n_y - 1]
    target = [
        (jnp.minimum(gx + 1, n_x - 1), gy), (jnp.maximum(gx - 1, 0), gy),
        (gx, jnp.minimum(gy + 1, n_y - 1)), (gx, jnp.maximum(gy - 1, 0)),
    ]

    def edge_copy(r, d):
        if d < 2:
            count = 1 if (d == 1 and r in (VOLTS, STRESS)) else 2
            src, dst = send_x.at[r, d, 0:count], recv_x.at[r, d, 0:count]
        else:
            src, dst = send_y.at[r, d - 2], recv_y.at[r, d - 2]
        return pltpu.make_async_remote_copy(
            src_ref=src, dst_ref=dst, send_sem=send_sem.at[r, d], recv_sem=recv_sem.at[r, d],
            device_id=target[d], device_id_type=MESH,
        )

    def start(r, axis):
        if r == VOLTS and axis == 0:
            pl.semaphore_wait(barrier, n_a - 1 + n_b - 1)
        for d in (2 * axis, 2 * axis + 1):
            @pl.when(to_has[d])
            def _():
                edge_copy(r, d).start()

    def arrive(r, axis):
        for d in (2 * axis, 2 * axis + 1):
            @pl.when(from_has[d])
            def _():
                edge_copy(r, d).wait_recv()

    for d in range(2):
        @pl.when(jnp.logical_not(from_has[d]))
        def _():
            for r in range(ROUNDS):
                recv_x[r, d] = jnp.full(recv_x.shape[2:], 1.0 if r == PARTIAL else 0.0, jnp.float32)

        @pl.when(jnp.logical_not(from_has[d + 2]))
        def _():
            for r in range(ROUNDS):
                recv_y[r, d] = jnp.full(recv_y.shape[2:], 1.0 if r == PARTIAL else 0.0, jnp.float32)

    moves[9].wait()
    is_y = [dirs[l] for l in range(layers)]
    pos = []
    seen_x, seen_y = jnp.int32(0), jnp.int32(half)
    for l in range(layers):
        pos.append(jnp.where(is_y[l] == 1, seen_y, seen_x))
        seen_y = seen_y + is_y[l]
        seen_x = seen_x + 1 - is_y[l]
    layer = []
    for k in range(layers):
        at = jnp.int32(0)
        for l in range(1, layers):
            at = at + jnp.where(pos[l] == k, l, 0)
        layer.append(at)

    def slot_of(want):
        at = jnp.int32(0)
        for k in range(1, layers):
            at = at + jnp.where(layer[k] == want, k, 0)
        return at

    below = [jnp.maximum(layer[k] - 1, 0) for k in range(layers)]
    above = [jnp.minimum(layer[k] + 1, layers - 1) for k in range(layers)]
    slot_below = [slot_of(below[k]) for k in range(layers)]
    slot_above = [slot_of(above[k]) for k in range(layers)]

    wide = rows_y // 2 if rows_y % 256 == 0 else rows_y
    tall = 8 if rows_x % 8 == 0 else rows_x
    cuts = [
        [(slice(0, rows_x), slice(j, j + wide)) for j in range(0, rows_y, wide)],
        [(slice(i, i + tall), slice(0, rows_y)) for i in range(0, rows_x, tall)],
    ]
    shapes = [(rows_x, wide), (tall, rows_y)]
    length = [rows_x, rows_y]
    index = [lax.broadcasted_iota(jnp.int32, shapes[axis], axis) for axis in range(2)]
    is_first = [index[axis] == 0 for axis in range(2)]
    is_last = [index[axis] == length[axis] - 1 for axis in range(2)]
    outer = [
        jnp.logical_and(is_last[0], gx == n_x - 1),
        jnp.logical_and(is_last[1], gy == n_y - 1),
    ]
    lane = lax.broadcasted_iota(jnp.int32, (tall, 128), 1)

    def pieces(send=None, recv=None):
        for axis in (0, 1) if recv is None else (1, 0):
            if recv is not None:
                arrive(recv, axis)
            for k in range(axis * half, axis * half + half):
                for rows, cols in cuts[axis]:
                    yield k, axis, (rows, cols)
            if send is not None:
                start(send, axis)

    def key(k, p):
        return k, p[0].start, p[1].start

    def take(ref, k, p):
        return ref[k, p[0], p[1]]

    def keep(ref, k, p, value):
        ref[k, p[0], p[1]] = value

    def before(a, h, axis):
        return jnp.where(is_first[axis], h, pltpu.roll(a, 1, axis))

    def after(a, h, axis):
        return jnp.where(is_last[axis], h, pltpu.roll(a, length[axis] - 1, axis))

    def first(a, axis):
        return a[0:1, :] if axis == 0 else a[:, 0:1]

    def last(a, axis):
        return a[rows_x - 1:rows_x, :] if axis == 0 else a[:, rows_y - 1:rows_y]

    def put(r, k, p, to_next, to_prev):
        for d, values in ((0, to_next), (1, to_prev)):
            if k < half:
                for i, value in enumerate(values):
                    send_x[r, d, i, k:k + 1, p[1]] = value
            else:
                packed = jnp.broadcast_to(values[0], (tall, 128))
                if len(values) > 1:
                    packed = jnp.where(lane == 0, packed, values[1])
                send_y[r, d, k - half, p[0], :] = packed

    def halo(r, k, p, d, i):
        if k < half:
            return recv_x[r, d, i, k:k + 1, p[1]]
        return recv_y[r, d, k - half, p[0], i:i + 1]

    def fold(a):
        r = a[0:8]
        for i in range(8, a.shape[0], 8):
            r = r + a[i:i + 8]
        out = r[:, 0:128]
        for j in range(128, a.shape[1], 128):
            out = out + r[:, j:j + 128]
        return out

    def sum_copy(leg, o, sender):
        group, me, n, sems = ((sum_a, me_a, n_a, (sa_send, sa_recv)), (sum_b, me_b, n_b, (sb_send, sb_recv)))[leg]
        slot = me if sender else lax.rem(me + o, n)
        return pltpu.make_async_remote_copy(
            src_ref=group.at[me], dst_ref=group.at[slot], send_sem=sems[0].at[o - 1], recv_sem=sems[1].at[slot],
            device_id=member(leg, o), device_id_type=MESH,
        )

    def first_leg():
        for o in range(1, n_a):
            sum_copy(0, o, False).wait_recv()
        along = sum_a[0]
        for i in range(1, n_a):
            along = along + sum_a[i]
        sum_b[me_b] = along
        for o in range(1, n_b):
            sum_copy(1, o, True).start()

    moves[0].wait()
    moves[1].wait()
    for k, axis, p in pieces(VOLTS):
        cr = jnp.where(outer[axis], 0.0, take(seg_in, layer[k], p))
        keep(cond, k, p, cr)
        v = take(volts_in, layer[k], p)
        put(VOLTS, k, p, [last(v, axis), last(cr, axis)], [first(v, axis)])

    def inside(axis, coef, field, minus=None):
        flux = coef * (pltpu.roll(field, length[axis] - 1, axis) - field)
        if minus is not None:
            flux = flux - minus
        flux = jnp.where(is_last[axis], 0.0, flux)
        return flux - pltpu.roll(flux, 1, axis)

    def upright(k, p, v, v_below, v_above):
        return take(via_b, k, p) * v_below + take(via_a, k, p) * v_above + take(source, k, p) - take(anchor, k, p) * v

    for move in moves[2:6]:
        move.wait()
    for move in moves[6:9]:
        move.start()
    for k, axis, p in pieces(PARTIAL):
        l = layer[k]
        up = jnp.minimum(l, layers - 2)
        va = take(via_in, up, p) * (take(vmask_in, up, p).astype(jnp.float32) * jnp.where(l < layers - 1, 1.0, 0.0))
        vb = take(via_in, below[k], p) * (take(vmask_in, below[k], p).astype(jnp.float32) * jnp.where(l > 0, 1.0, 0.0))
        pads = pad_conductance * pad_in[p[0], p[1]].astype(jnp.float32)
        top = pads * jnp.where(l == layers - 1, 1.0, 0.0)
        src = top * supply_volts - load_in[p[0], p[1]] * jnp.where(l == 0, 1.0, 0.0)
        hold = va + vb + top
        keep(via_a, k, p, va)
        keep(via_b, k, p, vb)
        keep(source, k, p, src)
        keep(anchor, k, p, hold)
        v = take(volts_in, l, p)
        cr = take(cond, k, p)
        dg = hold + cr + before(cr, 0.0, axis)
        res = inside(axis, cr, v) + vb * take(volts_in, below[k], p) + va * take(volts_in, above[k], p) + src - hold * v
        keep(diag, k, p, dg)
        keep(partial, k, p, res)
        put(PARTIAL, k, p, [last(res, axis), last(dg, axis)], [first(res, axis), first(dg, axis)])

    for move in moves[6:9]:
        move.wait()
    for k, axis, p in pieces(STRESS):
        l = layer[k]
        mr = jnp.where(outer[axis], 0.0, take(mob_in, l, p) * (1.0 - take(blk_in, l, p).astype(jnp.float32)))
        keep(mob, k, p, mr)
        s = take(stress_in, l, p)
        put(STRESS, k, p, [last(s, axis), last(mr, axis)], [first(s, axis)])

    def edge_next(k, p, v_prev, r_prev, v_next, r_next, v):
        axis = 0 if k < half else 1
        c_in, c_out = halo(VOLTS, k, p, 0, 1), last(take(cond, k, p), axis)
        h_prev = v_prev + damping * (r_prev + c_in * (first(v, axis) - v_prev)) / halo(PARTIAL, k, p, 0, 1)
        h_next = v_next + damping * (r_next + c_out * (last(v, axis) - v_next)) / (halo(PARTIAL, k, p, 1, 1) + c_out)
        return h_prev, h_next

    def edges(axis, at_first, at_last):
        return jnp.where(is_first[axis], at_first, jnp.where(is_last[axis], at_last, 0.0))

    for k, axis, p in pieces(recv=VOLTS):
        c_in, c_out = halo(VOLTS, k, p, 0, 1), last(take(cond, k, p), axis)
        v = take(volts_in, layer[k], p)
        w = damping / (take(diag, k, p) + jnp.where(is_first[axis], c_in, 0.0))
        keep(weight, k, p, w)
        cross = edges(
            axis, c_in * (halo(VOLTS, k, p, 0, 0) - first(v, axis)), c_out * (halo(VOLTS, k, p, 1, 0) - last(v, axis))
        )
        keep(volts_a, k, p, v + w * (take(partial, k, p) + cross))

    for k, axis, p in pieces(recv=PARTIAL):
        v = take(volts_a, k, p)
        h_prev, h_next = edge_next(
            k, p, halo(VOLTS, k, p, 0, 0), halo(PARTIAL, k, p, 0, 0), halo(VOLTS, k, p, 1, 0), halo(PARTIAL, k, p, 1, 0),
            take(volts_in, layer[k], p),
        )
        flux = take(cond, k, p) * (after(v, h_next, axis) - v)
        net = flux - before(flux, halo(VOLTS, k, p, 0, 1) * (first(v, axis) - h_prev), axis)
        keep(volts_b, k, p, v + take(weight, k, p) * (net + upright(k, p, v, take(volts_a, slot_below[k], p), take(volts_a, slot_above[k], p))))
    for k, axis, p in pieces(VOLTS2):
        v = take(volts_b, k, p)
        res = inside(axis, take(cond, k, p), v) + upright(k, p, v, take(volts_b, slot_below[k], p), take(volts_b, slot_above[k], p))
        keep(volts_a, k, p, v + take(weight, k, p) * res)
        put(VOLTS2, k, p, [last(v, axis), last(res, axis)], [first(v, axis), first(res, axis)])

    for k, axis, p in pieces(recv=STRESS):
        s = take(stress_in, layer[k], p)
        flux = take(mob, k, p) * (after(s, halo(STRESS, k, p, 1, 0), axis) - s)
        at_first = halo(STRESS, k, p, 0, 1) * (first(s, axis) - halo(STRESS, k, p, 0, 0))
        keep(stress_a, k, p, s + flux - before(flux, at_first, axis))

    entry, pull = {}, {}
    for k, axis, p in pieces(send=STRESS1, recv=VOLTS2):
        c_in, c_out = halo(VOLTS, k, p, 0, 1), last(take(cond, k, p), axis)
        v_prev, v_next, v = halo(VOLTS2, k, p, 0, 0), halo(VOLTS2, k, p, 1, 0), take(volts_b, k, p)
        h_prev, h_next = edge_next(k, p, v_prev, halo(VOLTS2, k, p, 0, 1), v_next, halo(VOLTS2, k, p, 1, 1), v)
        cross = edges(axis, c_in * (v_prev - first(v, axis)), c_out * (v_next - last(v, axis)))
        v = take(volts_a, k, p) + take(weight, k, p) * cross
        keep(volts_a, k, p, v)
        flux = take(cond, k, p) * (after(v, h_next, axis) - v)
        keep(partial, k, p, flux)
        at_first = c_in * (first(v, axis) - h_prev)
        mr = take(mob, k, p)
        wind = wind_factor * mr * flux
        keep(diag, k, p, wind)
        wind_first = wind_factor * halo(STRESS, k, p, 0, 1) * at_first
        entry[key(k, p)] = at_first
        pull[key(k, p)] = wind_first
        s = take(stress_a, k, p) - wind + before(wind, wind_first, axis)
        keep(stress_a, k, p, s)
        part = s + inside(axis, mr, s, wind)
        keep(stress_b, k, p, part)
        put(STRESS1, k, p, [last(s, axis), last(part, axis)], [first(s, axis), first(part, axis)])

    total = jnp.zeros((8, 128), jnp.float32)
    for k, axis, p in pieces():
        flux = take(partial, k, p)
        net = flux - before(flux, entry[key(k, p)], axis)
        res = net + upright(k, p, take(volts_a, k, p), take(volts_a, slot_below[k], p), take(volts_a, slot_above[k], p))
        total = total + fold(res * res)

    sum_a[me_a] = jnp.sum(total, axis=0, keepdims=True)
    for o in range(1, n_a):
        sum_copy(0, o, True).start()

    for l in range(layers):
        volts_fin[l] = volts_a[pos[l]]
    out_v = pltpu.make_async_copy(volts_fin, volts_out, out_sem.at[0])
    out_v.start()

    for k, axis, p in pieces(recv=STRESS1):
        mr, wind, s = take(mob, k, p), take(diag, k, p), take(stress_a, k, p)
        m_in, m_out = halo(STRESS, k, p, 0, 1), last(mr, axis)
        s_prev, s_next = halo(STRESS1, k, p, 0, 0), halo(STRESS1, k, p, 1, 0)
        flux_in = m_in * (first(s, axis) - s_prev) - pull[key(k, p)]
        flux_out = m_out * (s_next - last(s, axis)) - last(wind, axis)
        s = take(stress_b, k, p) + edges(axis, -flux_in, flux_out)
        h_prev = halo(STRESS1, k, p, 0, 1) + flux_in
        h_next = halo(STRESS1, k, p, 1, 1) - flux_out
        flux = mr * (after(s, h_next, axis) - s) - wind
        keep(stress_a, k, p, s + flux - before(flux, m_in * (first(s, axis) - h_prev) - pull[key(k, p)], axis))
        if n_b > 1 and k == layers - 1 and p == cuts[1][-1]:
            first_leg()
    for l in range(layers):
        stress_fin[l] = stress_a[pos[l]]
    out_s = pltpu.make_async_copy(stress_fin, stress_out, out_sem.at[1])
    out_s.start()

    if n_b == 1:
        first_leg()
    for o in range(1, n_b):
        sum_copy(1, o, False).wait_recv()
    whole = sum_b[0]
    for i in range(1, n_b):
        whole = whole + sum_b[i]
    nodes = layers * n_x * rows_x * n_y * rows_y
    mean = jnp.sum(whole, keepdims=True) * (1.0 / nodes)
    rms_out[0, 0] = jnp.sqrt(mean)[0, 0]

    for r in range(ROUNDS):
        for d in range(4):
            @pl.when(to_has[d])
            def _():
                edge_copy(r, d).wait_send()
    for leg, n in ((0, n_a), (1, n_b)):
        for o in range(1, n):
            sum_copy(leg, o, True).wait_send()
    out_v.wait()
    out_s.wait()


def deliver(volts_ref, stress_ref, volts_out, stress_out, sems):
    parts = sems.shape[1]
    count = volts_ref.shape[0] // parts
    moves = [
        pltpu.make_async_copy(src.at[i * count:(i + 1) * count], dst.at[i * count:(i + 1) * count], sems.at[j, i])
        for j, (src, dst) in enumerate([(volts_ref, volts_out), (stress_ref, stress_out)])
        for i in range(parts)
    ]
    for move in moves:
        move.start()
    for move in moves:
        move.wait()


def body(n_x, n_y, volts_start, seg_cond, via_cond, via_mask, pad_mask, load_current, stress_start, mobility, blocked, layer_dirs):
    layers, rows_x, rows_y = seg_cond.shape
    half = layers // 2
    n_a, n_b = (n_x * n_y, 1) if n_x * n_y <= 64 else (n_x, n_y)
    f32, i32 = jnp.float32, jnp.int32
    full = (layers, rows_x, rows_y)
    vias = via_cond.shape
    flat = (rows_x, rows_y)
    dma = pltpu.SemaphoreType.DMA
    out = pl.BlockSpec(memory_space=pl.ANY)
    hbm = pl.BlockSpec(memory_space=pltpu.HBM)
    operands = (
        layer_dirs, volts_start, seg_cond, via_cond, via_mask, pad_mask, load_current, stress_start, mobility, blocked
    )
    volts, stress, rms = pl.pallas_call(
        functools.partial(kernel, n_x, n_y, n_a, n_b, layers, rows_x, rows_y),
        out_shape=(
            jax.ShapeDtypeStruct(full, f32),
            jax.ShapeDtypeStruct(full, f32),
            jax.ShapeDtypeStruct((1, 1), f32),
        ),
        in_specs=[hbm] * 10,
        out_specs=(out, out, pl.BlockSpec(memory_space=pltpu.SMEM)),
        scratch_shapes=[
            pltpu.SMEM((layers,), i32),
            pltpu.VMEM(full, f32), pltpu.VMEM(full, f32), pltpu.VMEM(vias, f32), pltpu.VMEM(vias, i32),
            pltpu.VMEM(flat, i32), pltpu.VMEM(flat, f32), pltpu.VMEM(full, f32), pltpu.VMEM(full, f32), pltpu.VMEM(full, i32),
        ]
        + [pltpu.VMEM(full, f32)] * 15
        + [
            pltpu.VMEM((ROUNDS, 2, 2, half, rows_y), f32), pltpu.VMEM((ROUNDS, 2, 2, half, rows_y), f32),
            pltpu.VMEM((ROUNDS, 2, half, rows_x, 128), f32), pltpu.VMEM((ROUNDS, 2, half, rows_x, 128), f32),
            pltpu.VMEM((n_a, 1, 128), f32), pltpu.VMEM((n_b, 1, 128), f32),
            dma((10,)), dma((2,)), dma((ROUNDS, 4)), dma((ROUNDS, 4)),
            dma((n_a,)), dma((n_a,)), dma((n_b,)), dma((n_b,)),
        ],
        compiler_params=pltpu.CompilerParams(
            collective_id=0, has_side_effects=True, vmem_limit_bytes=40 * 1024 * 1024
        ),
        cost_estimate=pl.CostEstimate(flops=20_000_000, bytes_accessed=5_000_000, transcendentals=0),
    )(*[pltpu.with_memory_space_constraint(operand, pltpu.HBM) for operand in operands])
    volts, stress = pl.pallas_call(
        deliver,
        out_shape=(jax.ShapeDtypeStruct(full, f32), jax.ShapeDtypeStruct(full, f32)),
        in_specs=[out, out],
        out_specs=(hbm, hbm),
        scratch_shapes=[dma((2, 4))],
        compiler_params=pltpu.CompilerParams(vmem_limit_bytes=2 * 1024 * 1024),
        cost_estimate=pl.CostEstimate(flops=0, bytes_accessed=2_000_000, transcendentals=0),
    )(volts, stress)
    return volts, stress, rms.reshape(())


def solution(mesh):
    tile = P(None, "gx", "gy")
    flat = P("gx", "gy")
    in_specs = (tile, tile, tile, tile, flat, flat, tile, tile, tile, P())
    return jax.shard_map(
        functools.partial(body, mesh.shape["gx"], mesh.shape["gy"]),
        mesh=mesh, in_specs=in_specs, out_specs=(tile, tile, P()), check_vma=False,
    )
```

```python
import functools
import jax
import jax.numpy as jnp
from jax import lax
from jax.experimental import pallas as pl
from jax.experimental.pallas import tpu as pltpu
from jax.sharding import PartitionSpec as P

damping = 0.8
pad_conductance = 4.0
supply_volts = 1.0
wind_factor = 4.0

MESH = pl.DeviceIdType.MESH
VOLTS, STRESS, PARTIAL, VOLTS2, STRESS1 = range(5)
ROUNDS = 5


def kernel(
    n_x, n_y, n_a, n_b, layers, rows_x, rows_y,
    dirs_hbm, volts_hbm, seg_hbm, via_hbm, vmask_hbm, pad_hbm, load_hbm, stress_hbm, mob_hbm, blk_hbm,
    volts_out, stress_out, rms_out,
    dirs, volts_in, seg_in, via_in, vmask_in, pad_in, load_in, stress_in, mob_in, blk_in,
    cond, via_b, via_a, source, anchor, diag, weight, partial, mob, volts_a, volts_b, stress_a, stress_b,
    volts_fin, stress_fin,
    send_x, recv_x, send_y, recv_y, sum_a, sum_b,
    in_sem, out_sem, send_sem, recv_sem, sa_send, sa_recv, sb_send, sb_recv,
):
    half = layers // 2
    gx = lax.axis_index("gx")
    gy = lax.axis_index("gy")

    moves = [
        pltpu.make_async_copy(src, dst, in_sem.at[i])
        for i, (src, dst) in enumerate(
            [
                (volts_hbm, volts_in), (seg_hbm, seg_in), (via_hbm, via_in), (vmask_hbm, vmask_in), (pad_hbm, pad_in),
                (load_hbm, load_in), (stress_hbm, stress_in), (mob_hbm, mob_in), (blk_hbm, blk_in), (dirs_hbm, dirs),
            ]
        )
    ]
    moves[9].start()
    for move in moves[:6]:
        move.start()

    barrier = pltpu.get_barrier_semaphore()
    me_a, me_b = (gx, gy) if n_b > 1 else (gx * n_y + gy, 0)

    def member(leg, o):
        if leg == 1:
            return gx, lax.rem(gy + o, n_b)
        other = lax.rem(me_a + o, n_a)
        return (other, gy) if n_b > 1 else (other // n_y, lax.rem(other, n_y))

    for leg, n in ((0, n_a), (1, n_b)):
        for o in range(1, n):
            pl.semaphore_signal(barrier, inc=1, device_id=member(leg, o), device_id_type=MESH)

    to_has = [gx < n_x - 1, gx > 0, gy < n_y - 1, gy > 0]
    from_has = [gx > 0, gx < n_x - 1, gy > 0, gy < n_y - 1]
    target = [
        (jnp.minimum(gx + 1, n_x - 1), gy), (jnp.maximum(gx - 1, 0), gy),
        (gx, jnp.minimum(gy + 1, n_y - 1)), (gx, jnp.maximum(gy - 1, 0)),
    ]

    def edge_copy(r, d, i):
        if d < 2:
            src, dst, sem = send_x.at[r, d, i], recv_x.at[r, d, i], 2 * d + i
        else:
            src, dst, sem = send_y.at[r, d - 2], recv_y.at[r, d - 2], 2 + d
        return pltpu.make_async_remote_copy(
            src_ref=src, dst_ref=dst, send_sem=send_sem.at[r, sem], recv_sem=recv_sem.at[r, sem],
            device_id=target[d], device_id_type=MESH,
        )

    def copies(r, d):
        if d >= 2 or (d == 1 and r in (VOLTS, STRESS)):
            return (0,)
        return (0, 1)

    def start(r, axis, which=(0, 1)):
        if r == VOLTS and axis == 0:
            pl.semaphore_wait(barrier, n_a - 1 + n_b - 1)
        for d in (2 * axis, 2 * axis + 1):
            @pl.when(to_has[d])
            def _():
                for i in copies(r, d):
                    if axis == 1 or i in which:
                        edge_copy(r, d, i).start()

    def arrive(r, axis):
        for d in (2 * axis, 2 * axis + 1):
            @pl.when(from_has[d])
            def _():
                for i in copies(r, d):
                    edge_copy(r, d, i).wait_recv()

    for d in range(2):
        @pl.when(jnp.logical_not(from_has[d]))
        def _():
            for r in range(ROUNDS):
                recv_x[r, d] = jnp.full(recv_x.shape[2:], 1.0 if r == PARTIAL else 0.0, jnp.float32)

        @pl.when(jnp.logical_not(from_has[d + 2]))
        def _():
            for r in range(ROUNDS):
                recv_y[r, d] = jnp.full(recv_y.shape[2:], 1.0 if r == PARTIAL else 0.0, jnp.float32)

    moves[9].wait()
    is_y = [dirs[l] for l in range(layers)]
    pos = []
    seen_x, seen_y = jnp.int32(0), jnp.int32(half)
    for l in range(layers):
        pos.append(jnp.where(is_y[l] == 1, seen_y, seen_x))
        seen_y = seen_y + is_y[l]
        seen_x = seen_x + 1 - is_y[l]
    layer = []
    for k in range(layers):
        at = jnp.int32(0)
        for l in range(1, layers):
            at = at + jnp.where(pos[l] == k, l, 0)
        layer.append(at)

    def slot_of(want):
        at = jnp.int32(0)
        for k in range(1, layers):
            at = at + jnp.where(layer[k] == want, k, 0)
        return at

    below = [jnp.maximum(layer[k] - 1, 0) for k in range(layers)]
    above = [jnp.minimum(layer[k] + 1, layers - 1) for k in range(layers)]
    slot_below = [slot_of(below[k]) for k in range(layers)]
    slot_above = [slot_of(above[k]) for k in range(layers)]

    wide = rows_y // 2 if rows_y % 256 == 0 else rows_y
    tall = 8 if rows_x % 8 == 0 else rows_x
    cuts = [
        [(slice(0, rows_x), slice(j, j + wide)) for j in range(0, rows_y, wide)],
        [(slice(i, i + tall), slice(0, rows_y)) for i in range(0, rows_x, tall)],
    ]
    shapes = [(rows_x, wide), (tall, rows_y)]
    length = [rows_x, rows_y]
    index = [lax.broadcasted_iota(jnp.int32, shapes[axis], axis) for axis in range(2)]
    is_first = [index[axis] == 0 for axis in range(2)]
    is_last = [index[axis] == length[axis] - 1 for axis in range(2)]
    outer = [
        jnp.logical_and(is_last[0], gx == n_x - 1),
        jnp.logical_and(is_last[1], gy == n_y - 1),
    ]
    lane = lax.broadcasted_iota(jnp.int32, (tall, 128), 1)

    def pieces_of(axis):
        for k in range(axis * half, axis * half + half):
            for rows, cols in cuts[axis]:
                yield k, axis, (rows, cols)

    def pieces(send=None, recv=None, which=(0, 1)):
        for axis in (0, 1) if recv is None else (1, 0):
            if recv is not None:
                arrive(recv, axis)
            yield from pieces_of(axis)
            if send is not None:
                start(send, axis, which)

    def key(k, p):
        return k, p[0].start, p[1].start

    def take(ref, k, p):
        return ref[k, p[0], p[1]]

    def keep(ref, k, p, value):
        ref[k, p[0], p[1]] = value

    def before(a, h, axis):
        return jnp.where(is_first[axis], h, pltpu.roll(a, 1, axis))

    def after(a, h, axis):
        return jnp.where(is_last[axis], h, pltpu.roll(a, length[axis] - 1, axis))

    def first(a, axis):
        return a[0:1, :] if axis == 0 else a[:, 0:1]

    def last(a, axis):
        return a[rows_x - 1:rows_x, :] if axis == 0 else a[:, rows_y - 1:rows_y]

    def put(r, k, p, to_next, to_prev, base=0):
        for d, values in ((0, to_next), (1, to_prev)):
            if k < half:
                for i, value in enumerate(values):
                    send_x[r, d, base + i, k:k + 1, p[1]] = value
            else:
                packed = jnp.broadcast_to(values[0], (tall, 128))
                if len(values) > 1:
                    packed = jnp.where(lane == 0, packed, values[1])
                send_y[r, d, k - half, p[0], :] = packed

    def halo(r, k, p, d, i):
        if k < half:
            return recv_x[r, d, i, k:k + 1, p[1]]
        return recv_y[r, d, k - half, p[0], i:i + 1]

    def fold(a):
        r = a[0:8]
        for i in range(8, a.shape[0], 8):
            r = r + a[i:i + 8]
        out = r[:, 0:128]
        for j in range(128, a.shape[1], 128):
            out = out + r[:, j:j + 128]
        return out

    def sum_copy(leg, o, sender):
        group, me, n, sems = ((sum_a, me_a, n_a, (sa_send, sa_recv)), (sum_b, me_b, n_b, (sb_send, sb_recv)))[leg]
        slot = me if sender else lax.rem(me + o, n)
        return pltpu.make_async_remote_copy(
            src_ref=group.at[me], dst_ref=group.at[slot], send_sem=sems[0].at[o - 1], recv_sem=sems[1].at[slot],
            device_id=member(leg, o), device_id_type=MESH,
        )

    def first_leg():
        for o in range(1, n_a):
            sum_copy(0, o, False).wait_recv()
        along = sum_a[0]
        for i in range(1, n_a):
            along = along + sum_a[i]
        sum_b[me_b] = along
        for o in range(1, n_b):
            sum_copy(1, o, True).start()

    moves[0].wait()
    moves[1].wait()
    for k, axis, p in pieces(VOLTS):
        cr = jnp.where(outer[axis], 0.0, take(seg_in, layer[k], p))
        keep(cond, k, p, cr)
        v = take(volts_in, layer[k], p)
        put(VOLTS, k, p, [last(v, axis), last(cr, axis)], [first(v, axis)])

    def inside(axis, coef, field, minus=None):
        flux = coef * (pltpu.roll(field, length[axis] - 1, axis) - field)
        if minus is not None:
            flux = flux - minus
        flux = jnp.where(is_last[axis], 0.0, flux)
        return flux - pltpu.roll(flux, 1, axis)

    def upright(k, p, v, v_below, v_above):
        return take(via_b, k, p) * v_below + take(via_a, k, p) * v_above + take(source, k, p) - take(anchor, k, p) * v

    for move in moves[2:6]:
        move.wait()
    for move in moves[6:9]:
        move.start()
    for along in (0, 1):
        for k, axis, p in pieces_of(along):
            l = layer[k]
            up = jnp.minimum(l, layers - 2)
            va = take(via_in, up, p) * (take(vmask_in, up, p).astype(jnp.float32) * jnp.where(l < layers - 1, 1.0, 0.0))
            vb = take(via_in, below[k], p) * (take(vmask_in, below[k], p).astype(jnp.float32) * jnp.where(l > 0, 1.0, 0.0))
            pads = pad_conductance * pad_in[p[0], p[1]].astype(jnp.float32)
            top = pads * jnp.where(l == layers - 1, 1.0, 0.0)
            src = top * supply_volts - load_in[p[0], p[1]] * jnp.where(l == 0, 1.0, 0.0)
            hold = va + vb + top
            keep(via_a, k, p, va)
            keep(via_b, k, p, vb)
            keep(source, k, p, src)
            keep(anchor, k, p, hold)
            cr = take(cond, k, p)
            dg = hold + cr + before(cr, 0.0, axis)
            keep(diag, k, p, dg)
            if axis == 0:
                put(PARTIAL, k, p, [last(dg, axis)], [first(dg, axis)], 1)
        if along == 0:
            start(PARTIAL, 0, (1,))
        for k, axis, p in pieces_of(along):
            l = layer[k]
            v, cr, dg = take(volts_in, l, p), take(cond, k, p), take(diag, k, p)
            va, vb, src, hold = take(via_a, k, p), take(via_b, k, p), take(source, k, p), take(anchor, k, p)
            res = inside(axis, cr, v) + vb * take(volts_in, below[k], p) + va * take(volts_in, above[k], p) + src - hold * v
            keep(partial, k, p, res)
            if axis == 0:
                put(PARTIAL, k, p, [last(res, axis)], [first(res, axis)])
            else:
                put(PARTIAL, k, p, [last(res, axis), last(dg, axis)], [first(res, axis), first(dg, axis)])
        start(PARTIAL, along, (0,))

    for move in moves[6:9]:
        move.wait()
    for k, axis, p in pieces(STRESS):
        l = layer[k]
        mr = jnp.where(outer[axis], 0.0, take(mob_in, l, p) * (1.0 - take(blk_in, l, p).astype(jnp.float32)))
        keep(mob, k, p, mr)
        s = take(stress_in, l, p)
        put(STRESS, k, p, [last(s, axis), last(mr, axis)], [first(s, axis)])

    def edge_next(k, p, v_prev, r_prev, v_next, r_next, v):
        axis = 0 if k < half else 1
        c_in, c_out = halo(VOLTS, k, p, 0, 1), last(take(cond, k, p), axis)
        h_prev = v_prev + damping * (r_prev + c_in * (first(v, axis) - v_prev)) / halo(PARTIAL, k, p, 0, 1)
        h_next = v_next + damping * (r_next + c_out * (last(v, axis) - v_next)) / (halo(PARTIAL, k, p, 1, 1) + c_out)
        return h_prev, h_next

    def edges(axis, at_first, at_last):
        return jnp.where(is_first[axis], at_first, jnp.where(is_last[axis], at_last, 0.0))

    for k, axis, p in pieces(recv=VOLTS):
        c_in, c_out = halo(VOLTS, k, p, 0, 1), last(take(cond, k, p), axis)
        v = take(volts_in, layer[k], p)
        w = damping / (take(diag, k, p) + jnp.where(is_first[axis], c_in, 0.0))
        keep(weight, k, p, w)
        cross = edges(
            axis, c_in * (halo(VOLTS, k, p, 0, 0) - first(v, axis)), c_out * (halo(VOLTS, k, p, 1, 0) - last(v, axis))
        )
        keep(volts_a, k, p, v + w * (take(partial, k, p) + cross))

    for k, axis, p in pieces(recv=PARTIAL):
        v = take(volts_a, k, p)
        h_prev, h_next = edge_next(
            k, p, halo(VOLTS, k, p, 0, 0), halo(PARTIAL, k, p, 0, 0), halo(VOLTS, k, p, 1, 0), halo(PARTIAL, k, p, 1, 0),
            take(volts_in, layer[k], p),
        )
        flux = take(cond, k, p) * (after(v, h_next, axis) - v)
        net = flux - before(flux, halo(VOLTS, k, p, 0, 1) * (first(v, axis) - h_prev), axis)
        net = net + upright(k, p, v, take(volts_a, slot_below[k], p), take(volts_a, slot_above[k], p))
        v = v + take(weight, k, p) * net
        keep(volts_b, k, p, v)
        if axis == 0:
            put(VOLTS2, k, p, [last(v, axis)], [first(v, axis)])
    start(VOLTS2, 0, (0,))
    for k, axis, p in pieces(VOLTS2, which=(1,)):
        v = take(volts_b, k, p)
        res = inside(axis, take(cond, k, p), v) + upright(k, p, v, take(volts_b, slot_below[k], p), take(volts_b, slot_above[k], p))
        keep(volts_a, k, p, v + take(weight, k, p) * res)
        if axis == 0:
            put(VOLTS2, k, p, [last(res, axis)], [first(res, axis)], 1)
        else:
            put(VOLTS2, k, p, [last(v, axis), last(res, axis)], [first(v, axis), first(res, axis)])

    for k, axis, p in pieces(recv=STRESS):
        s = take(stress_in, layer[k], p)
        flux = take(mob, k, p) * (after(s, halo(STRESS, k, p, 1, 0), axis) - s)
        at_first = halo(STRESS, k, p, 0, 1) * (first(s, axis) - halo(STRESS, k, p, 0, 0))
        keep(stress_a, k, p, s + flux - before(flux, at_first, axis))

    entry, pull = {}, {}
    for k, axis, p in pieces(send=STRESS1, recv=VOLTS2, which=(0,)):
        c_in, c_out = halo(VOLTS, k, p, 0, 1), last(take(cond, k, p), axis)
        v_prev, v_next, v = halo(VOLTS2, k, p, 0, 0), halo(VOLTS2, k, p, 1, 0), take(volts_b, k, p)
        h_prev, h_next = edge_next(k, p, v_prev, halo(VOLTS2, k, p, 0, 1), v_next, halo(VOLTS2, k, p, 1, 1), v)
        cross = edges(axis, c_in * (v_prev - first(v, axis)), c_out * (v_next - last(v, axis)))
        v = take(volts_a, k, p) + take(weight, k, p) * cross
        keep(volts_a, k, p, v)
        flux = take(cond, k, p) * (after(v, h_next, axis) - v)
        keep(partial, k, p, flux)
        at_first = c_in * (first(v, axis) - h_prev)
        mr = take(mob, k, p)
        wind = wind_factor * mr * flux
        keep(diag, k, p, wind)
        wind_first = wind_factor * halo(STRESS, k, p, 0, 1) * at_first
        entry[key(k, p)] = at_first
        pull[key(k, p)] = wind_first
        s = take(stress_a, k, p) - wind + before(wind, wind_first, axis)
        keep(stress_a, k, p, s)
        if axis == 0:
            put(STRESS1, k, p, [last(s, axis)], [first(s, axis)])
            continue
        part = s + inside(axis, mr, s, wind)
        keep(stress_b, k, p, part)
        put(STRESS1, k, p, [last(s, axis), last(part, axis)], [first(s, axis), first(part, axis)])
    for k, axis, p in pieces_of(0):
        s = take(stress_a, k, p)
        part = s + inside(axis, take(mob, k, p), s, take(diag, k, p))
        keep(stress_b, k, p, part)
        put(STRESS1, k, p, [last(part, axis)], [first(part, axis)], 1)
    start(STRESS1, 0, (1,))

    total = jnp.zeros((8, 128), jnp.float32)
    for k, axis, p in pieces():
        flux = take(partial, k, p)
        net = flux - before(flux, entry[key(k, p)], axis)
        res = net + upright(k, p, take(volts_a, k, p), take(volts_a, slot_below[k], p), take(volts_a, slot_above[k], p))
        total = total + fold(res * res)

    sum_a[me_a] = jnp.sum(total, axis=0, keepdims=True)
    for o in range(1, n_a):
        sum_copy(0, o, True).start()

    for l in range(layers):
        volts_fin[l] = volts_a[pos[l]]
    out_v = pltpu.make_async_copy(volts_fin, volts_out, out_sem.at[0])
    out_v.start()

    for k, axis, p in pieces(recv=STRESS1):
        mr, wind, s = take(mob, k, p), take(diag, k, p), take(stress_a, k, p)
        m_in, m_out = halo(STRESS, k, p, 0, 1), last(mr, axis)
        s_prev, s_next = halo(STRESS1, k, p, 0, 0), halo(STRESS1, k, p, 1, 0)
        flux_in = m_in * (first(s, axis) - s_prev) - pull[key(k, p)]
        flux_out = m_out * (s_next - last(s, axis)) - last(wind, axis)
        s = take(stress_b, k, p) + edges(axis, -flux_in, flux_out)
        h_prev = halo(STRESS1, k, p, 0, 1) + flux_in
        h_next = halo(STRESS1, k, p, 1, 1) - flux_out
        flux = mr * (after(s, h_next, axis) - s) - wind
        keep(stress_a, k, p, s + flux - before(flux, m_in * (first(s, axis) - h_prev) - pull[key(k, p)], axis))
        if n_b > 1 and k == layers - 1 and p == cuts[1][-1]:
            first_leg()
    out_s = []
    for l in range(0, layers, 2):
        stress_fin[l] = stress_a[pos[l]]
        stress_fin[l + 1] = stress_a[pos[l + 1]]
        out_s.append(pltpu.make_async_copy(stress_fin.at[l:l + 2], stress_out.at[l:l + 2], out_sem.at[1 + l // 2]))
        out_s[-1].start()

    if n_b == 1:
        first_leg()
    for o in range(1, n_b):
        sum_copy(1, o, False).wait_recv()
    whole = sum_b[0]
    for i in range(1, n_b):
        whole = whole + sum_b[i]
    nodes = layers * n_x * rows_x * n_y * rows_y
    mean = jnp.sum(whole, keepdims=True) * (1.0 / nodes)
    rms_out[0, 0] = jnp.sqrt(mean)[0, 0]

    for r in range(ROUNDS):
        for d in range(4):
            @pl.when(to_has[d])
            def _():
                for i in copies(r, d):
                    edge_copy(r, d, i).wait_send()
    for leg, n in ((0, n_a), (1, n_b)):
        for o in range(1, n):
            sum_copy(leg, o, True).wait_send()
    out_v.wait()
    for move in out_s:
        move.wait()


def deliver(volts_ref, stress_ref, volts_out, stress_out, sems):
    parts = sems.shape[1]
    count = volts_ref.shape[0] // parts
    moves = [
        pltpu.make_async_copy(src.at[i * count:(i + 1) * count], dst.at[i * count:(i + 1) * count], sems.at[j, i])
        for j, (src, dst) in enumerate([(volts_ref, volts_out), (stress_ref, stress_out)])
        for i in range(parts)
    ]
    for move in moves:
        move.start()
    for move in moves:
        move.wait()


def body(n_x, n_y, volts_start, seg_cond, via_cond, via_mask, pad_mask, load_current, stress_start, mobility, blocked, layer_dirs):
    layers, rows_x, rows_y = seg_cond.shape
    half = layers // 2
    n_a, n_b = (n_x * n_y, 1) if n_x * n_y <= 64 else (n_x, n_y)
    f32, i32 = jnp.float32, jnp.int32
    full = (layers, rows_x, rows_y)
    vias = via_cond.shape
    flat = (rows_x, rows_y)
    dma = pltpu.SemaphoreType.DMA
    out = pl.BlockSpec(memory_space=pl.ANY)
    hbm = pl.BlockSpec(memory_space=pltpu.HBM)
    operands = (
        layer_dirs, volts_start, seg_cond, via_cond, via_mask, pad_mask, load_current, stress_start, mobility, blocked
    )
    volts, stress, rms = pl.pallas_call(
        functools.partial(kernel, n_x, n_y, n_a, n_b, layers, rows_x, rows_y),
        out_shape=(
            jax.ShapeDtypeStruct(full, f32),
            jax.ShapeDtypeStruct(full, f32),
            jax.ShapeDtypeStruct((1, 1), f32),
        ),
        in_specs=[hbm] * 10,
        out_specs=(out, out, pl.BlockSpec(memory_space=pltpu.SMEM)),
        scratch_shapes=[
            pltpu.SMEM((layers,), i32),
            pltpu.VMEM(full, f32), pltpu.VMEM(full, f32), pltpu.VMEM(vias, f32), pltpu.VMEM(vias, i32),
            pltpu.VMEM(flat, i32), pltpu.VMEM(flat, f32), pltpu.VMEM(full, f32), pltpu.VMEM(full, f32), pltpu.VMEM(full, i32),
        ]
        + [pltpu.VMEM(full, f32)] * 15
        + [
            pltpu.VMEM((ROUNDS, 2, 2, half, rows_y), f32), pltpu.VMEM((ROUNDS, 2, 2, half, rows_y), f32),
            pltpu.VMEM((ROUNDS, 2, half, rows_x, 128), f32), pltpu.VMEM((ROUNDS, 2, half, rows_x, 128), f32),
            pltpu.VMEM((n_a, 1, 128), f32), pltpu.VMEM((n_b, 1, 128), f32),
            dma((10,)), dma((1 + half,)), dma((ROUNDS, 6)), dma((ROUNDS, 6)),
            dma((n_a,)), dma((n_a,)), dma((n_b,)), dma((n_b,)),
        ],
        compiler_params=pltpu.CompilerParams(
            collective_id=0, has_side_effects=True, vmem_limit_bytes=40 * 1024 * 1024
        ),
        cost_estimate=pl.CostEstimate(flops=20_000_000, bytes_accessed=5_000_000, transcendentals=0),
    )(*[pltpu.with_memory_space_constraint(operand, pltpu.HBM) for operand in operands])
    volts, stress = pl.pallas_call(
        deliver,
        out_shape=(jax.ShapeDtypeStruct(full, f32), jax.ShapeDtypeStruct(full, f32)),
        in_specs=[out, out],
        out_specs=(hbm, hbm),
        scratch_shapes=[dma((2, 4))],
        compiler_params=pltpu.CompilerParams(vmem_limit_bytes=2 * 1024 * 1024),
        cost_estimate=pl.CostEstimate(flops=0, bytes_accessed=2_000_000, transcendentals=0),
    )(volts, stress)
    return volts, stress, rms.reshape(())


def solution(mesh):
    tile = P(None, "gx", "gy")
    flat = P("gx", "gy")
    in_specs = (tile, tile, tile, tile, flat, flat, tile, tile, tile, P())
    return jax.shard_map(
        functools.partial(body, mesh.shape["gx"], mesh.shape["gy"]),
        mesh=mesh, in_specs=in_specs, out_specs=(tile, tile, P()), check_vma=False,
    )
```

```python
import functools
import jax
import jax.numpy as jnp
from jax import lax
from jax.experimental import pallas as pl
from jax.experimental.pallas import tpu as pltpu
from jax.sharding import PartitionSpec as P

damping = 0.8
pad_conductance = 4.0
supply_volts = 1.0
wind_factor = 4.0

MESH = pl.DeviceIdType.MESH
VOLTS, STRESS, PARTIAL, VOLTS2, STRESS1 = range(5)
ROUNDS = 5


def kernel(
    n_x, n_y, n_a, n_b, layers, rows_x, rows_y,
    dirs_hbm, volts_hbm, seg_hbm, via_hbm, vmask_hbm, pad_hbm, load_hbm, stress_hbm, mob_hbm, blk_hbm,
    volts_out, stress_out, rms_out,
    dirs, volts_in, seg_in, via_in, vmask_in, pad_in, load_in, stress_in, mob_in, blk_in,
    cond, via_b, via_a, source, anchor, diag, weight, partial, mob, volts_a, volts_b, stress_a, stress_b,
    volts_fin, stress_fin,
    send_x, recv_x, send_y, recv_y, sum_a, sum_b,
    in_sem, out_sem, send_sem, recv_sem, sa_send, sa_recv, sb_send, sb_recv,
):
    half = layers // 2
    gx = lax.axis_index("gx")
    gy = lax.axis_index("gy")

    moves = [
        pltpu.make_async_copy(src, dst, in_sem.at[i])
        for i, (src, dst) in enumerate(
            [
                (volts_hbm, volts_in), (seg_hbm, seg_in), (via_hbm, via_in), (vmask_hbm, vmask_in), (pad_hbm, pad_in),
                (load_hbm, load_in), (stress_hbm, stress_in), (mob_hbm, mob_in), (blk_hbm, blk_in), (dirs_hbm, dirs),
            ]
        )
    ]
    moves[9].start()
    for move in moves[:6]:
        move.start()

    barrier = pltpu.get_barrier_semaphore()
    me_a, me_b = (gx, gy) if n_b > 1 else (gx * n_y + gy, 0)

    def member(leg, o):
        if leg == 1:
            return gx, lax.rem(gy + o, n_b)
        other = lax.rem(me_a + o, n_a)
        return (other, gy) if n_b > 1 else (other // n_y, lax.rem(other, n_y))

    for leg, n in ((0, n_a), (1, n_b)):
        for o in range(1, n):
            pl.semaphore_signal(barrier, inc=1, device_id=member(leg, o), device_id_type=MESH)

    to_has = [gx < n_x - 1, gx > 0, gy < n_y - 1, gy > 0]
    from_has = [gx > 0, gx < n_x - 1, gy > 0, gy < n_y - 1]
    target = [
        (jnp.minimum(gx + 1, n_x - 1), gy), (jnp.maximum(gx - 1, 0), gy),
        (gx, jnp.minimum(gy + 1, n_y - 1)), (gx, jnp.maximum(gy - 1, 0)),
    ]

    def edge_copy(r, d):
        if d < 2:
            count = 1 if (d == 1 and r in (VOLTS, STRESS)) else 2
            src, dst = send_x.at[r, d, 0:count], recv_x.at[r, d, 0:count]
        else:
            src, dst = send_y.at[r, d - 2], recv_y.at[r, d - 2]
        return pltpu.make_async_remote_copy(
            src_ref=src, dst_ref=dst, send_sem=send_sem.at[r, d], recv_sem=recv_sem.at[r, d],
            device_id=target[d], device_id_type=MESH,
        )

    def start(r, axis):
        if r == VOLTS and axis == 0:
            pl.semaphore_wait(barrier, n_a - 1 + n_b - 1)
        for d in (2 * axis, 2 * axis + 1):
            @pl.when(to_has[d])
            def _():
                edge_copy(r, d).start()

    def arrive(r, axis):
        for d in (2 * axis, 2 * axis + 1):
            @pl.when(from_has[d])
            def _():
                edge_copy(r, d).wait_recv()

    def sent(r):
        for d in range(4):
            @pl.when(to_has[d])
            def _():
                edge_copy(r, d).wait_send()

    for d in range(2):
        @pl.when(jnp.logical_not(from_has[d]))
        def _():
            for r in range(ROUNDS):
                recv_x[r, d] = jnp.full(recv_x.shape[2:], 1.0 if r == PARTIAL else 0.0, jnp.float32)

        @pl.when(jnp.logical_not(from_has[d + 2]))
        def _():
            for r in range(ROUNDS):
                recv_y[r, d] = jnp.full(recv_y.shape[2:], 1.0 if r == PARTIAL else 0.0, jnp.float32)

    moves[9].wait()
    is_y = [dirs[l] for l in range(layers)]
    pos = []
    seen_x, seen_y = jnp.int32(0), jnp.int32(half)
    for l in range(layers):
        pos.append(jnp.where(is_y[l] == 1, seen_y, seen_x))
        seen_y = seen_y + is_y[l]
        seen_x = seen_x + 1 - is_y[l]
    layer = []
    for k in range(layers):
        at = jnp.int32(0)
        for l in range(1, layers):
            at = at + jnp.where(pos[l] == k, l, 0)
        layer.append(at)

    def slot_of(want):
        at = jnp.int32(0)
        for k in range(1, layers):
            at = at + jnp.where(layer[k] == want, k, 0)
        return at

    below = [jnp.maximum(layer[k] - 1, 0) for k in range(layers)]
    above = [jnp.minimum(layer[k] + 1, layers - 1) for k in range(layers)]
    slot_below = [slot_of(below[k]) for k in range(layers)]
    slot_above = [slot_of(above[k]) for k in range(layers)]

    wide = rows_y // 2 if rows_y % 256 == 0 else rows_y
    tall = 8 if rows_x % 8 == 0 else rows_x
    cuts = [
        [(slice(0, rows_x), slice(j, j + wide)) for j in range(0, rows_y, wide)],
        [(slice(i, i + tall), slice(0, rows_y)) for i in range(0, rows_x, tall)],
    ]
    shapes = [(rows_x, wide), (tall, rows_y)]
    length = [rows_x, rows_y]
    index = [lax.broadcasted_iota(jnp.int32, shapes[axis], axis) for axis in range(2)]
    is_first = [index[axis] == 0 for axis in range(2)]
    is_last = [index[axis] == length[axis] - 1 for axis in range(2)]
    outer = [
        jnp.logical_and(is_last[0], gx == n_x - 1),
        jnp.logical_and(is_last[1], gy == n_y - 1),
    ]
    lane = lax.broadcasted_iota(jnp.int32, (tall, 128), 1)

    def pieces(send=None, recv=None):
        for axis in (0, 1) if recv is None else (1, 0):
            if recv is not None:
                arrive(recv, axis)
            for k in range(axis * half, axis * half + half):
                for rows, cols in cuts[axis]:
                    yield k, axis, (rows, cols)
            if send is not None:
                start(send, axis)

    def key(k, p):
        return k, p[0].start, p[1].start

    def take(ref, k, p):
        return ref[k, p[0], p[1]]

    def keep(ref, k, p, value):
        ref[k, p[0], p[1]] = value

    def before(a, h, axis):
        return jnp.where(is_first[axis], h, pltpu.roll(a, 1, axis))

    def after(a, h, axis):
        return jnp.where(is_last[axis], h, pltpu.roll(a, length[axis] - 1, axis))

    def first(a, axis):
        return a[0:1, :] if axis == 0 else a[:, 0:1]

    def last(a, axis):
        return a[rows_x - 1:rows_x, :] if axis == 0 else a[:, rows_y - 1:rows_y]

    def put(r, k, p, to_next, to_prev):
        for d, values in ((0, to_next), (1, to_prev)):
            if k < half:
                for i, value in enumerate(values):
                    send_x[r, d, i, k:k + 1, p[1]] = value
            else:
                packed = jnp.broadcast_to(values[0], (tall, 128))
                if len(values) > 1:
                    packed = jnp.where(lane == 0, packed, values[1])
                send_y[r, d, k - half, p[0], :] = packed

    def halo(r, k, p, d, i):
        if k < half:
            return recv_x[r, d, i, k:k + 1, p[1]]
        return recv_y[r, d, k - half, p[0], i:i + 1]

    def fold(a):
        r = a[0:8]
        for i in range(8, a.shape[0], 8):
            r = r + a[i:i + 8]
        out = r[:, 0:128]
        for j in range(128, a.shape[1], 128):
            out = out + r[:, j:j + 128]
        return out

    def sum_copy(leg, o, sender):
        group, me, n, sems = ((sum_a, me_a, n_a, (sa_send, sa_recv)), (sum_b, me_b, n_b, (sb_send, sb_recv)))[leg]
        slot = me if sender else lax.rem(me + o, n)
        return pltpu.make_async_remote_copy(
            src_ref=group.at[me], dst_ref=group.at[slot], send_sem=sems[0].at[o - 1], recv_sem=sems[1].at[slot],
            device_id=member(leg, o), device_id_type=MESH,
        )

    def first_leg():
        for o in range(1, n_a):
            sum_copy(0, o, False).wait_recv()
        along = sum_a[0]
        for i in range(1, n_a):
            along = along + sum_a[i]
        sum_b[me_b] = along
        for o in range(1, n_b):
            sum_copy(1, o, True).start()

    moves[0].wait()
    moves[1].wait()
    for k, axis, p in pieces(VOLTS):
        cr = jnp.where(outer[axis], 0.0, take(seg_in, layer[k], p))
        keep(cond, k, p, cr)
        v = take(volts_in, layer[k], p)
        put(VOLTS, k, p, [last(v, axis), last(cr, axis)], [first(v, axis)])

    def inside(axis, coef, field, minus=None):
        flux = coef * (pltpu.roll(field, length[axis] - 1, axis) - field)
        if minus is not None:
            flux = flux - minus
        flux = jnp.where(is_last[axis], 0.0, flux)
        return flux - pltpu.roll(flux, 1, axis)

    def upright(k, p, v, v_below, v_above):
        return take(via_b, k, p) * v_below + take(via_a, k, p) * v_above + take(source, k, p) - take(anchor, k, p) * v

    for move in moves[2:6]:
        move.wait()
    for move in moves[6:9]:
        move.start()
    for k, axis, p in pieces(PARTIAL):
        l = layer[k]
        up = jnp.minimum(l, layers - 2)
        va = take(via_in, up, p) * (take(vmask_in, up, p).astype(jnp.float32) * jnp.where(l < layers - 1, 1.0, 0.0))
        vb = take(via_in, below[k], p) * (take(vmask_in, below[k], p).astype(jnp.float32) * jnp.where(l > 0, 1.0, 0.0))
        pads = pad_conductance * pad_in[p[0], p[1]].astype(jnp.float32)
        top = pads * jnp.where(l == layers - 1, 1.0, 0.0)
        src = top * supply_volts - load_in[p[0], p[1]] * jnp.where(l == 0, 1.0, 0.0)
        hold = va + vb + top
        keep(via_a, k, p, va)
        keep(via_b, k, p, vb)
        keep(source, k, p, src)
        keep(anchor, k, p, hold)
        v = take(volts_in, l, p)
        cr = take(cond, k, p)
        dg = hold + cr + before(cr, 0.0, axis)
        res = inside(axis, cr, v) + vb * take(volts_in, below[k], p) + va * take(volts_in, above[k], p) + src - hold * v
        keep(diag, k, p, dg)
        keep(partial, k, p, res)
        put(PARTIAL, k, p, [last(res, axis), last(dg, axis)], [first(res, axis), first(dg, axis)])

    for move in moves[6:9]:
        move.wait()
    for k, axis, p in pieces(STRESS):
        l = layer[k]
        mr = jnp.where(outer[axis], 0.0, take(mob_in, l, p) * (1.0 - take(blk_in, l, p).astype(jnp.float32)))
        keep(mob, k, p, mr)
        s = take(stress_in, l, p)
        put(STRESS, k, p, [last(s, axis), last(mr, axis)], [first(s, axis)])

    def edge_next(k, p, v_prev, r_prev, v_next, r_next, v):
        axis = 0 if k < half else 1
        c_in, c_out = halo(VOLTS, k, p, 0, 1), last(take(cond, k, p), axis)
        h_prev = v_prev + damping * (r_prev + c_in * (first(v, axis) - v_prev)) / halo(PARTIAL, k, p, 0, 1)
        h_next = v_next + damping * (r_next + c_out * (last(v, axis) - v_next)) / (halo(PARTIAL, k, p, 1, 1) + c_out)
        return h_prev, h_next

    def edges(axis, at_first, at_last):
        return jnp.where(is_first[axis], at_first, jnp.where(is_last[axis], at_last, 0.0))

    for k, axis, p in pieces(recv=VOLTS):
        c_in, c_out = halo(VOLTS, k, p, 0, 1), last(take(cond, k, p), axis)
        v = take(volts_in, layer[k], p)
        w = damping / (take(diag, k, p) + jnp.where(is_first[axis], c_in, 0.0))
        keep(weight, k, p, w)
        cross = edges(
            axis, c_in * (halo(VOLTS, k, p, 0, 0) - first(v, axis)), c_out * (halo(VOLTS, k, p, 1, 0) - last(v, axis))
        )
        keep(volts_a, k, p, v + w * (take(partial, k, p) + cross))

    for k, axis, p in pieces(recv=PARTIAL):
        v = take(volts_a, k, p)
        h_prev, h_next = edge_next(
            k, p, halo(VOLTS, k, p, 0, 0), halo(PARTIAL, k, p, 0, 0), halo(VOLTS, k, p, 1, 0), halo(PARTIAL, k, p, 1, 0),
            take(volts_in, layer[k], p),
        )
        flux = take(cond, k, p) * (after(v, h_next, axis) - v)
        net = flux - before(flux, halo(VOLTS, k, p, 0, 1) * (first(v, axis) - h_prev), axis)
        keep(volts_b, k, p, v + take(weight, k, p) * (net + upright(k, p, v, take(volts_a, slot_below[k], p), take(volts_a, slot_above[k], p))))
    for k, axis, p in pieces(VOLTS2):
        v = take(volts_b, k, p)
        res = inside(axis, take(cond, k, p), v) + upright(k, p, v, take(volts_b, slot_below[k], p), take(volts_b, slot_above[k], p))
        keep(volts_a, k, p, v + take(weight, k, p) * res)
        put(VOLTS2, k, p, [last(v, axis), last(res, axis)], [first(v, axis), first(res, axis)])

    for k, axis, p in pieces(recv=STRESS):
        s = take(stress_in, layer[k], p)
        flux = take(mob, k, p) * (after(s, halo(STRESS, k, p, 1, 0), axis) - s)
        at_first = halo(STRESS, k, p, 0, 1) * (first(s, axis) - halo(STRESS, k, p, 0, 0))
        keep(stress_a, k, p, s + flux - before(flux, at_first, axis))

    entry, pull = {}, {}
    for k, axis, p in pieces(send=STRESS1, recv=VOLTS2):
        c_in, c_out = halo(VOLTS, k, p, 0, 1), last(take(cond, k, p), axis)
        v_prev, v_next, v = halo(VOLTS2, k, p, 0, 0), halo(VOLTS2, k, p, 1, 0), take(volts_b, k, p)
        h_prev, h_next = edge_next(k, p, v_prev, halo(VOLTS2, k, p, 0, 1), v_next, halo(VOLTS2, k, p, 1, 1), v)
        cross = edges(axis, c_in * (v_prev - first(v, axis)), c_out * (v_next - last(v, axis)))
        v = take(volts_a, k, p) + take(weight, k, p) * cross
        keep(volts_a, k, p, v)
        flux = take(cond, k, p) * (after(v, h_next, axis) - v)
        keep(partial, k, p, flux)
        at_first = c_in * (first(v, axis) - h_prev)
        mr = take(mob, k, p)
        wind = wind_factor * mr * flux
        keep(diag, k, p, wind)
        wind_first = wind_factor * halo(STRESS, k, p, 0, 1) * at_first
        entry[key(k, p)] = at_first
        pull[key(k, p)] = wind_first
        s = take(stress_a, k, p) - wind + before(wind, wind_first, axis)
        keep(stress_a, k, p, s)
        part = s + inside(axis, mr, s, wind)
        keep(stress_b, k, p, part)
        put(STRESS1, k, p, [last(s, axis), last(part, axis)], [first(s, axis), first(part, axis)])

    total = jnp.zeros((8, 128), jnp.float32)
    for k, axis, p in pieces():
        flux = take(partial, k, p)
        net = flux - before(flux, entry[key(k, p)], axis)
        res = net + upright(k, p, take(volts_a, k, p), take(volts_a, slot_below[k], p), take(volts_a, slot_above[k], p))
        total = total + fold(res * res)

    sum_a[me_a] = jnp.sum(total, axis=0, keepdims=True)
    for o in range(1, n_a):
        sum_copy(0, o, True).start()

    for l in range(layers):
        volts_fin[l] = volts_a[pos[l]]
    out_v = pltpu.make_async_copy(volts_fin, volts_out, out_sem.at[0])
    out_v.start()

    for r in (VOLTS, PARTIAL, STRESS, VOLTS2):
        sent(r)

    for k, axis, p in pieces(recv=STRESS1):
        mr, wind, s = take(mob, k, p), take(diag, k, p), take(stress_a, k, p)
        m_in, m_out = halo(STRESS, k, p, 0, 1), last(mr, axis)
        s_prev, s_next = halo(STRESS1, k, p, 0, 0), halo(STRESS1, k, p, 1, 0)
        flux_in = m_in * (first(s, axis) - s_prev) - pull[key(k, p)]
        flux_out = m_out * (s_next - last(s, axis)) - last(wind, axis)
        s = take(stress_b, k, p) + edges(axis, -flux_in, flux_out)
        h_prev = halo(STRESS1, k, p, 0, 1) + flux_in
        h_next = halo(STRESS1, k, p, 1, 1) - flux_out
        flux = mr * (after(s, h_next, axis) - s) - wind
        keep(stress_a, k, p, s + flux - before(flux, m_in * (first(s, axis) - h_prev) - pull[key(k, p)], axis))
        if n_b > 1 and k == layers - 1 and p == cuts[1][-1]:
            first_leg()
    out_s = []
    for l in range(0, layers, 2):
        stress_fin[l] = stress_a[pos[l]]
        stress_fin[l + 1] = stress_a[pos[l + 1]]
        out_s.append(pltpu.make_async_copy(stress_fin.at[l:l + 2], stress_out.at[l:l + 2], out_sem.at[1 + l // 2]))
        out_s[-1].start()

    if n_b == 1:
        first_leg()
    for o in range(1, n_b):
        sum_copy(1, o, False).wait_recv()
    whole = sum_b[0]
    for i in range(1, n_b):
        whole = whole + sum_b[i]
    nodes = layers * n_x * rows_x * n_y * rows_y
    mean = jnp.sum(whole, keepdims=True) * (1.0 / nodes)
    rms_out[0, 0] = jnp.sqrt(mean)[0, 0]

    sent(STRESS1)
    for leg, n in ((0, n_a), (1, n_b)):
        for o in range(1, n):
            sum_copy(leg, o, True).wait_send()
    out_v.wait()
    for move in out_s:
        move.wait()


def deliver(volts_ref, stress_ref, volts_out, stress_out, sems):
    parts = sems.shape[1]
    count = volts_ref.shape[0] // parts
    moves = [
        pltpu.make_async_copy(src.at[i * count:(i + 1) * count], dst.at[i * count:(i + 1) * count], sems.at[j, i])
        for j, (src, dst) in enumerate([(volts_ref, volts_out), (stress_ref, stress_out)])
        for i in range(parts)
    ]
    for move in moves:
        move.start()
    for move in moves:
        move.wait()


def body(n_x, n_y, volts_start, seg_cond, via_cond, via_mask, pad_mask, load_current, stress_start, mobility, blocked, layer_dirs):
    layers, rows_x, rows_y = seg_cond.shape
    half = layers // 2
    n_a, n_b = (n_x * n_y, 1) if n_x * n_y <= 64 else (n_x, n_y)
    f32, i32 = jnp.float32, jnp.int32
    full = (layers, rows_x, rows_y)
    vias = via_cond.shape
    flat = (rows_x, rows_y)
    dma = pltpu.SemaphoreType.DMA
    out = pl.BlockSpec(memory_space=pl.ANY)
    hbm = pl.BlockSpec(memory_space=pltpu.HBM)
    operands = (
        layer_dirs, volts_start, seg_cond, via_cond, via_mask, pad_mask, load_current, stress_start, mobility, blocked
    )
    volts, stress, rms = pl.pallas_call(
        functools.partial(kernel, n_x, n_y, n_a, n_b, layers, rows_x, rows_y),
        out_shape=(
            jax.ShapeDtypeStruct(full, f32),
            jax.ShapeDtypeStruct(full, f32),
            jax.ShapeDtypeStruct((1, 1), f32),
        ),
        in_specs=[hbm] * 10,
        out_specs=(out, out, pl.BlockSpec(memory_space=pltpu.SMEM)),
        scratch_shapes=[
            pltpu.SMEM((layers,), i32),
            pltpu.VMEM(full, f32), pltpu.VMEM(full, f32), pltpu.VMEM(vias, f32), pltpu.VMEM(vias, i32),
            pltpu.VMEM(flat, i32), pltpu.VMEM(flat, f32), pltpu.VMEM(full, f32), pltpu.VMEM(full, f32), pltpu.VMEM(full, i32),
        ]
        + [pltpu.VMEM(full, f32)] * 15
        + [
            pltpu.VMEM((ROUNDS, 2, 2, half, rows_y), f32), pltpu.VMEM((ROUNDS, 2, 2, half, rows_y), f32),
            pltpu.VMEM((ROUNDS, 2, half, rows_x, 128), f32), pltpu.VMEM((ROUNDS, 2, half, rows_x, 128), f32),
            pltpu.VMEM((n_a, 1, 128), f32), pltpu.VMEM((n_b, 1, 128), f32),
            dma((10,)), dma((1 + half,)), dma((ROUNDS, 4)), dma((ROUNDS, 4)),
            dma((n_a,)), dma((n_a,)), dma((n_b,)), dma((n_b,)),
        ],
        compiler_params=pltpu.CompilerParams(
            collective_id=0, has_side_effects=True, vmem_limit_bytes=40 * 1024 * 1024
        ),
        cost_estimate=pl.CostEstimate(flops=20_000_000, bytes_accessed=5_000_000, transcendentals=0),
    )(*[pltpu.with_memory_space_constraint(operand, pltpu.HBM) for operand in operands])
    volts, stress = pl.pallas_call(
        deliver,
        out_shape=(jax.ShapeDtypeStruct(full, f32), jax.ShapeDtypeStruct(full, f32)),
        in_specs=[out, out],
        out_specs=(hbm, hbm),
        scratch_shapes=[dma((2, 4))],
        compiler_params=pltpu.CompilerParams(vmem_limit_bytes=2 * 1024 * 1024),
        cost_estimate=pl.CostEstimate(flops=0, bytes_accessed=2_000_000, transcendentals=0),
    )(volts, stress)
    return volts, stress, rms.reshape(())


def solution(mesh):
    tile = P(None, "gx", "gy")
    flat = P("gx", "gy")
    in_specs = (tile, tile, tile, tile, flat, flat, tile, tile, tile, P())
    return jax.shard_map(
        functools.partial(body, mesh.shape["gx"], mesh.shape["gy"]),
        mesh=mesh, in_specs=in_specs, out_specs=(tile, tile, P()), check_vma=False,
    )
```
